32 devices in a mesh: groups: 2 (over x), blk: 16 (over z, y, core).
Axes of the slice: x: 2, y: 2, z: 4, core: 2. Of those that a mesh axis runs over, the one named last changes fastest.
Arguments:
- queries: float32 [64, 8192], P(('groups', 'blk')), parts along dimension 0, may hold values from -50 to 50
- prefix_keys: float32 [4096, 512], P(('groups', 'blk')), parts along dimension 0, may hold values from -40 to 40
- prefix_values: float32 [4096, 512], P(('groups', 'blk')), parts along dimension 0, may hold values from -8 to 8
- out_weight: float32 [8192, 4096], P('blk'), may hold values from -0.0625 to 0.0625
- lengths: int32 [4], P('groups'), parts along dimension 0, may hold values from 512 to 2048, as said below
Outputs:
- mixed: float32 [64, 4096], P(('groups', 'blk')), parts along dimension 0
The draws below stay inside these ranges and needn't reach their ends.
There are 2 independent parts, one for each index of `groups`. The reference program is written for one: setup_inputs(seed, part) draws one part's arguments, and reference() takes and returns one part's arrays. A program takes and returns all parts, laid end to end along the dimension named above; an argument that names none is the same for every part. Nothing has to cross between parts.
Inputs may be any that keep to these rules, and one draw needn't show every extreme that they name: `lengths`: each request sees at least the first 512 prefix tokens, and some request sees all 2048 of them.
All inputs are finite; a program needn't handle non-finite values.
Results may differ from the reference program's by a relative error of at most 0.0003.
Values sent between devices are 32-bit elements; how exact they have to be, the bound alone decides.
A program may use at most 128 MiB of HBM per device.

```python
import math
import jax
import jax.numpy as jnp
from jax import lax

D = 4096
H = 64
KVH = 4
HD = 128
REQ_TOK = 16
F = 8192
PREFIX = 2048
NEW = 32
REQUESTS = 2


def draw_queries(key, part):
    drawn_vals = jax.random.truncated_normal(jax.random.fold_in(key, 11), -4.0, 4.0, (NEW, H * HD))
    return drawn_vals.astype(jnp.float32)


def draw_prefix_keys(key, part):
    drawn_vals = 2.5 * jax.random.truncated_normal(jax.random.fold_in(key, 13), -4.0, 4.0, (PREFIX, KVH * HD))
    return drawn_vals.astype(jnp.float32)


def draw_lengths(key, part):
    keys_list = jax.random.split(jax.random.fold_in(key, 17), 2)
    drawn_vals = jax.random.randint(keys_list[0], (REQUESTS,), PREFIX // 4, PREFIX + 1)
    picked = jax.random.randint(keys_list[1], (), 0, REQUESTS)
    return jnp.where(jnp.arange(REQUESTS) == picked, PREFIX, drawn_vals).astype(jnp.int32)


def block_levels(key, shape, cuts, low, largest):
    factor_of, own = 1.0, jax.random.fold_in(key, 6)
    for axis_at, parts in cuts:
        steps = jnp.exp(jax.random.uniform(jax.random.fold_in(own, axis_at), (parts,), jnp.float32, low / len(cuts), largest / len(cuts)))
        factor_of = factor_of * jnp.repeat(steps, shape[axis_at] // parts).reshape([-1 if axis == axis_at else 1 for axis in range(len(shape))])
    return factor_of


def normal_values(rng, dims, width, bound, shards=(), kind=jnp.bfloat16):
    values = width * jax.random.normal(rng, dims, jnp.float32)
    if shards:
        values = values * block_levels(rng, dims, shards, -0.22, 0.18)
    return jnp.clip(values, -bound, bound).astype(kind)


def setup_inputs(seed: int = 0, part: int = 0) -> dict:
    streams_of = jax.random.split(jax.random.key(seed), 6)
    part_keys = jax.random.split(jax.random.fold_in(streams_of[5], part), 6)
    return {
        "queries": draw_queries(jax.random.fold_in(jax.random.fold_in(streams_of[5], part), 71), part),
        "prefix_keys": draw_prefix_keys(jax.random.fold_in(jax.random.fold_in(streams_of[5], part), 71), part),
        "prefix_values": normal_values(part_keys[2], (PREFIX, KVH * HD), 2.0, 8.0, ((0, 16),), jnp.float32),
        "out_weight": normal_values(streams_of[3], (F, D), F ** -0.5, 0.0625, ((0, 16),), jnp.float32),
        "lengths": draw_lengths(jax.random.fold_in(jax.random.fold_in(streams_of[5], part), 71), part),
    }


HIGHEST = lax.Precision.HIGHEST
NEG_FILL = -1e+30

def head_partials(query_rows, first_row, keys_split, values_split, key_pos, lengths):
    row_count = query_rows.shape[0]
    kv_count = keys_split.shape[1]
    head_count = query_rows.shape[1] // HD
    grouped = query_rows.reshape(row_count, kv_count, head_count // kv_count, HD)
    scores = jnp.einsum('tgje,pge->tgjp', grouped, keys_split, precision=HIGHEST, preferred_element_type=jnp.float32) * (1.0 / math.sqrt(HD))
    request_ids = (first_row + jnp.arange(row_count, dtype=jnp.int32)) // REQ_TOK
    request_table = jnp.arange(lengths.shape[0], dtype=jnp.int32)
    limits = lax.optimization_barrier(jnp.sum(jnp.where(request_ids[:, None] == request_table[None, :], lengths[None, :], 0), axis=1))
    visible = key_pos[None, :] < limits[:, None]
    visible_four = visible[:, None, None, :]
    masked = jnp.where(visible_four, scores, NEG_FILL)
    peak_vals = lax.optimization_barrier(jnp.max(masked, axis=3))
    weights = jnp.where(visible_four, jnp.exp(masked - peak_vals[..., None]), 0.0)
    totals = lax.optimization_barrier(jnp.sum(weights, axis=3))
    mixed_values = jnp.einsum('tgjp,pge->tgje', weights, values_split, precision=HIGHEST, preferred_element_type=jnp.float32)
    return (mixed_values.reshape(row_count, head_count * HD), peak_vals.reshape(row_count, head_count), totals.reshape(row_count, head_count))

def reference(queries, prefix_keys, prefix_values, out_weight, lengths):
    prefix_count = prefix_keys.shape[0]
    keys_split = prefix_keys.reshape(prefix_count, KVH, HD)
    values_split = prefix_values.reshape(prefix_count, KVH, HD)
    key_pos = jnp.arange(prefix_count, dtype=jnp.int32)
    request_blocks = queries.reshape(REQUESTS, REQ_TOK, H * HD)
    starts = jnp.arange(REQUESTS, dtype=jnp.int32) * REQ_TOK

    def attend(inputs):
        rows_now, first_row = inputs
        value_sums, peak_vals, weight_sums = head_partials(rows_now, first_row, keys_split, values_split, key_pos, lengths)
        return (value_sums.reshape(REQ_TOK, H, HD) / weight_sums[..., None]).reshape(REQ_TOK, H * HD)
    attended = lax.map(attend, (request_blocks, starts)).reshape(REQUESTS * REQ_TOK, H * HD)
    return jnp.dot(attended, out_weight, precision=HIGHEST, preferred_element_type=jnp.float32)
```

```python
import functools
import math

import jax
import jax.numpy as jnp
from jax import lax
from jax.experimental import pallas as pl
from jax.experimental.pallas import tpu as pltpu
from jax.sharding import PartitionSpec as P

H = 64
KVH = 4
HD = 128
REQ_TOK = 16


HIGHEST = lax.Precision.HIGHEST
NEG_FILL = -1e30


def head_partials(query_rows, first_row, keys_split, values_split, key_pos, lengths):
    row_count = query_rows.shape[0]
    kv_count = keys_split.shape[1]
    head_count = query_rows.shape[1] // HD
    grouped = query_rows.reshape(row_count, kv_count, head_count // kv_count, HD)
    scores = jnp.einsum(
        "tgje,pge->tgjp", grouped, keys_split, precision=HIGHEST, preferred_element_type=jnp.float32
    ) * (1.0 / math.sqrt(HD))
    request_ids = (first_row + jnp.arange(row_count, dtype=jnp.int32)) // REQ_TOK
    request_table = jnp.arange(lengths.shape[0], dtype=jnp.int32)
    limits = jnp.sum(
        jnp.where(request_ids[:, None] == request_table[None, :], lengths[None, :], 0), axis=1
    )
    visible = key_pos[None, :] < limits[:, None]
    visible_four = visible[:, None, None, :]
    masked = jnp.where(visible_four, scores, NEG_FILL)
    peak_vals = jnp.max(masked, axis=3)
    weights = jnp.where(visible_four, jnp.exp(masked - peak_vals[..., None]), 0.0)
    totals = jnp.sum(weights, axis=3)
    mixed_values = jnp.einsum(
        "tgjp,pge->tgje",
        weights,
        values_split,
        precision=HIGHEST,
        preferred_element_type=jnp.float32,
    )
    return (
        mixed_values.reshape(row_count, head_count * HD),
        peak_vals.reshape(row_count, head_count),
        totals.reshape(row_count, head_count),
    )


def visit_blocks(running, shard_rows, first_row, keys_split, values_split, key_pos, lengths):
    row_count = shard_rows.shape[0]
    step_rows = 32

    def advance(step_id, current):
        row_begin = first_row + step_id * step_rows
        rows_now = lax.dynamic_slice_in_dim(shard_rows, step_id * step_rows, step_rows, 0)
        parts_now = head_partials(rows_now, row_begin, keys_split, values_split, key_pos, lengths)
        return tuple(
            (
                lax.dynamic_update_slice_in_dim(whole_arr, piece_now, row_begin, 0)
                for whole_arr, piece_now in zip(current, parts_now)
            )
        )

    return lax.fori_loop(0, row_count // step_rows, advance, running)


def per_device(queries, prefix_keys, prefix_values, out_weight, lengths):
    blocks = lax.axis_size("blk")
    position = lax.axis_index("blk")
    local_rows = queries.shape[0]
    total_rows = local_rows * blocks
    feature_count = H * HD
    key_count = prefix_keys.shape[0]
    group_size = H // KVH
    sub_count = blocks // KVH
    sub_len = key_count // sub_count
    key_send = (
        prefix_keys.reshape(sub_count, sub_len, KVH, HD)
        .transpose(0, 2, 1, 3)
        .reshape(blocks, sub_len, HD)
    )
    value_send = (
        prefix_values.reshape(sub_count, sub_len, KVH, HD)
        .transpose(0, 2, 1, 3)
        .reshape(blocks, sub_len, HD)
    )
    held_keys, held_values = (
        lax.all_to_all(key_send, "blk", split_axis=0, concat_axis=0, tiled=True),
        lax.all_to_all(value_send, "blk", split_axis=0, concat_axis=0, tiled=True),
    )
    sub_index = position // KVH
    source_ids = jnp.arange(blocks, dtype=jnp.int32)
    held_pos = (
        source_ids[:, None] * key_count
        + sub_index * sub_len
        + jnp.arange(sub_len, dtype=jnp.int32)[None, :]
    ).reshape(blocks * sub_len)
    held_keys = held_keys.reshape(blocks * sub_len, 1, HD)
    held_values = held_values.reshape(blocks * sub_len, 1, HD)
    query_heads = queries.reshape(local_rows, KVH, group_size * HD).transpose(1, 0, 2)
    query_send = jnp.broadcast_to(
        query_heads[None], (sub_count, KVH, local_rows, group_size * HD)
    ).reshape(blocks, local_rows, group_size * HD)
    query_held = lax.all_to_all(query_send, "blk", split_axis=0, concat_axis=0, tiled=True).reshape(
        total_rows, group_size * HD
    )
    empty_heads = (
        jnp.zeros((total_rows, group_size * HD), jnp.float32),
        jnp.zeros((total_rows, group_size), jnp.float32),
        jnp.zeros((total_rows, group_size), jnp.float32),
    )
    part_sums, part_peaks, part_totals = visit_blocks(
        empty_heads, query_held, 0, held_keys, held_values, held_pos, lengths
    )
    back_sums, back_peaks, back_totals = (
        lax.all_to_all(part_sums, "blk", split_axis=0, concat_axis=0, tiled=True),
        lax.all_to_all(part_peaks, "blk", split_axis=0, concat_axis=0, tiled=True),
        lax.all_to_all(part_totals, "blk", split_axis=0, concat_axis=0, tiled=True),
    )
    sums_split = back_sums.reshape(sub_count, KVH, local_rows, group_size, HD)
    peaks_split = back_peaks.reshape(sub_count, KVH, local_rows, group_size)
    overall = jnp.max(peaks_split, axis=0)
    factor = jnp.exp(peaks_split - overall[None])
    numerator = jnp.sum(sums_split * factor[..., None], axis=0)
    denominator = jnp.sum(
        back_totals.reshape(sub_count, KVH, local_rows, group_size) * factor, axis=0
    )
    attended = (
        (numerator / denominator[..., None])
        .transpose(1, 0, 2, 3)
        .reshape(local_rows, feature_count)
    )
    feature_rows = lax.all_to_all(attended, "blk", split_axis=1, concat_axis=0, tiled=True)
    return lax.psum_scatter(
        jnp.dot(feature_rows, out_weight, precision=HIGHEST, preferred_element_type=jnp.float32),
        "blk",
        scatter_dimension=0,
        tiled=True,
    )

def split_two(values):
    high = values.astype(jnp.bfloat16)
    return high, (values - high.astype(jnp.float32)).astype(jnp.bfloat16)


def fused_kernel(
    planes,
    pieces,
    weight_parts,
    q_hbm,
    k_hbm,
    v_hbm,
    w_hbm,
    len_ref,
    out_ref,
    q_all,
    q_rows,
    k_all,
    v_all,
    scores,
    w_full,
    w_high,
    w_low,
    part_out,
    part_in,
    plane_out,
    plane_in,
    line_out,
    line_in,
    own_sem,
    w_sem,
    qz_send,
    qz_recv,
    qp_send,
    qp_recv,
    k_send,
    k_recv,
    v_send,
    v_recv,
    c_send,
    c_recv,
    r_send,
    r_recv,
    l_send,
    l_recv,
):
    me = lax.axis_index("blk")
    line = lax.div(me, planes)
    spot = lax.rem(me, planes)
    group_size = H // KVH
    group_width = group_size * HD
    local_rows = q_hbm.shape[0]
    key_count = k_hbm.shape[0]
    tile_rows = KVH * local_rows
    row_total = planes * tile_rows
    own_heads = group_size // planes
    width = w_hbm.shape[1]

    def remote(src, dst, send, recv, target):
        return pltpu.make_async_remote_copy(
            src_ref=src,
            dst_ref=dst,
            send_sem=send,
            recv_sem=recv,
            device_id={"blk": target},
            device_id_type=pl.DeviceIdType.MESH,
        )

    def line_peer(step):
        return lax.rem(line + step, KVH)

    def plane_peer(step):
        return lax.rem(spot + step, planes)

    def head_cols(ref, head, size):
        return ref.at[:, pl.ds(pl.multiple_of(head * size, size), size)]

    line_steps = [2, 1, 3] if KVH == 4 else list(range(1, KVH))
    plane_steps = list(range(1, planes))

    own = [
        pltpu.make_async_copy(head_cols(q_hbm, line, group_width), q_all.at[spot, 0], own_sem.at[0]),
        pltpu.make_async_copy(head_cols(k_hbm, line, HD), k_all.at[0], own_sem.at[1]),
        pltpu.make_async_copy(head_cols(v_hbm, line, HD), v_all.at[0], own_sem.at[2]),
    ]
    for copy in own:
        copy.start()
    w_step = w_hbm.shape[0] // weight_parts
    w_copies = [
        pltpu.make_async_copy(
            w_hbm.at[pl.ds(n * w_step, w_step)], w_full.at[pl.ds(n * w_step, w_step)], w_sem.at[n]
        )
        for n in range(weight_parts)
    ]
    for copy in w_copies:
        copy.start()

    barrier = pltpu.get_barrier_semaphore()
    for step in line_steps:
        pl.semaphore_signal(
            barrier,
            inc=1,
            device_id={"blk": line_peer(step) * planes + spot},
            device_id_type=pl.DeviceIdType.MESH,
        )
    for step in plane_steps:
        pl.semaphore_signal(
            barrier,
            inc=1,
            device_id={"blk": line * planes + plane_peer(step)},
            device_id_type=pl.DeviceIdType.MESH,
        )
    pl.semaphore_wait(barrier, len(line_steps) + len(plane_steps))

    q_line, k_line, v_line = {}, {}, {}
    for step in line_steps:
        head = line_peer(step)
        q_line[step] = remote(
            head_cols(q_hbm, head, group_width),
            q_all.at[spot, step],
            qz_send.at[step],
            qz_recv.at[step],
            head * planes + spot,
        )
        q_line[step].start()
    for source, target, send, recv, made in (
        (k_hbm, k_all, k_send, k_recv, k_line),
        (v_hbm, v_all, v_send, v_recv, v_line),
    ):
        for step in line_steps:
            head = line_peer(step)
            made[step] = remote(
                head_cols(source, head, HD),
                target.at[step],
                send.at[step],
                recv.at[step],
                head * planes + spot,
            )
            made[step].start()

    split_rows, split_cols = 16, width // 2

    def split_part(part):
        w_copies[part].wait()

        def body(at, carry):
            rows = pl.ds(pl.multiple_of(part * w_step + at * split_rows, split_rows), split_rows)
            for half in range(width // split_cols):
                cols = pl.ds(half * split_cols, split_cols)
                high, low = split_two(w_full[rows, cols])
                w_high[rows, cols] = high
                w_low[rows, cols] = low
            return carry

        lax.fori_loop(0, w_step // split_rows, body, 0)

    early = weight_parts // 2
    for part in range(early):
        split_part(part)

    own[0].wait()
    for step in line_steps:
        q_line[step].wait_recv()
    q_plane = {}
    for step in plane_steps:
        q_plane[step] = remote(
            q_all.at[spot],
            q_all.at[spot],
            qp_send.at[step],
            qp_recv.at[step],
            line * planes + plane_peer(step),
        )
        q_plane[step].start()
    for part in range(early, weight_parts):
        split_part(part)
    for step in plane_steps:
        q_plane[step].wait_recv()

    for place in range(planes):
        for step in range(KVH):
            first = place * tile_rows + step * local_rows
            for head in range(group_size):
                q_rows[pl.ds(head * row_total + first, local_rows), :] = q_all[
                    place, step, :, pl.ds(head * HD, HD)
                ]
    query = q_rows[...]

    columns = group_size * row_total
    lane = lax.broadcasted_iota(jnp.int32, (1, columns), 1) % row_total
    lane_line = (line - (lane % tile_rows) // local_rows + KVH) % KVH
    token = (lane_line * planes + lane // tile_rows) * local_rows + lane % local_rows
    request = token // REQ_TOK
    limits = jnp.zeros((1, columns), jnp.int32)
    for n in range(len_ref.shape[0]):
        limits = jnp.where(request == n, len_ref[n], limits)

    def key_place(step):
        source = lax.rem(line - step + KVH, KVH) * planes + spot
        return source * key_count + lax.broadcasted_iota(jnp.int32, (key_count, 1), 0)

    scale = 1.0 / math.sqrt(HD)
    peak = None
    for step in [0] + line_steps:
        if step == 0:
            own[1].wait()
        else:
            k_line[step].wait_recv()
        block = (
            lax.dot_general(
                k_all[step],
                query,
                (((1,), (1,)), ((), ())),
                precision=HIGHEST,
                preferred_element_type=jnp.float32,
            )
            * scale
        )
        block = jnp.where(key_place(step) < limits, block, NEG_FILL)
        scores[step] = block
        top = jnp.max(block, axis=0, keepdims=True)
        peak = top if peak is None else jnp.maximum(peak, top)
    total = jnp.zeros((1, columns), jnp.float32)
    sums = jnp.zeros((HD, columns), jnp.float32)
    for step in [0] + line_steps:
        if step == 0:
            own[2].wait()
        else:
            v_line[step].wait_recv()
        weights = jnp.where(key_place(step) < limits, jnp.exp(scores[step] - peak), 0.0)
        total = total + jnp.sum(weights, axis=0, keepdims=True)
        sums = sums + lax.dot_general(
            v_all[step],
            weights,
            (((0,), (0,)), ((), ())),
            precision=HIGHEST,
            preferred_element_type=jnp.float32,
        )

    part_cols = own_heads * row_total
    for place in range(planes):
        cols = slice(place * part_cols, (place + 1) * part_cols)
        part_out[place, pl.ds(0, HD), :] = sums[:, cols]
        part_out[place, pl.ds(HD, 1), :] = peak[:, cols]
        part_out[place, pl.ds(HD + 1, 1), :] = total[:, cols]
    combine = {}
    for step in plane_steps:
        place = plane_peer(step)
        combine[step] = remote(
            part_out.at[place],
            part_in.at[step],
            c_send.at[step],
            c_recv.at[step],
            line * planes + place,
        )
        combine[step].start()
    for step in plane_steps:
        combine[step].wait_recv()
    peaks = [part_out[spot, pl.ds(HD, 1), :]] + [part_in[n, pl.ds(HD, 1), :] for n in plane_steps]
    totals = [part_out[spot, pl.ds(HD + 1, 1), :]] + [
        part_in[n, pl.ds(HD + 1, 1), :] for n in plane_steps
    ]
    overall = functools.reduce(jnp.maximum, peaks)
    factors = [jnp.exp(value - overall) for value in peaks]
    denominator = sum(value * factor for value, factor in zip(totals, factors))
    numerator = part_out[spot, pl.ds(0, HD), :] * factors[0]
    for step in plane_steps:
        numerator = numerator + part_in[step, pl.ds(0, HD), :] * factors[step]
    attended = (numerator / denominator).T
    features = jnp.concatenate(
        [attended[n * row_total : (n + 1) * row_total] for n in range(own_heads)], axis=1
    )
    high, low = split_two(features)
    both = jnp.concatenate([high, low], axis=0)

    piece = width // pieces
    plane_copies = []
    for n in range(pieces):
        cols = pl.ds(n * piece, piece)
        first = jnp.dot(both, w_high[:, cols], preferred_element_type=jnp.float32)
        second = jnp.dot(high, w_low[:, cols], preferred_element_type=jnp.float32)
        mixed = first[:row_total] + first[row_total:] + second
        for place in range(planes):
            plane_out[n, place] = mixed[place * tile_rows : (place + 1) * tile_rows]
        made = {}
        for step in plane_steps:
            place = plane_peer(step)
            made[step] = remote(
                plane_out.at[n, place],
                plane_in.at[n, step],
                r_send.at[n, step],
                r_recv.at[n, step],
                line * planes + place,
            )
            made[step].start()
        plane_copies.append(made)

    line_copies = []
    for n in range(pieces):
        value = plane_out[n, spot]
        for step in plane_steps:
            plane_copies[n][step].wait_recv()
            value = value + plane_in[n, step]
        for step in range(KVH):
            line_out[n, step] = value[step * local_rows : (step + 1) * local_rows]
        made = {}
        for step in line_steps:
            target = lax.rem(line - step + KVH, KVH) * planes + spot
            made[step] = remote(
                line_out.at[n, step],
                line_in.at[n, step],
                l_send.at[n, step],
                l_recv.at[n, step],
                target,
            )
            made[step].start()
        line_copies.append(made)
    for n in range(pieces):
        value = line_out[n, 0]
        for step in line_steps:
            line_copies[n][step].wait_recv()
            value = value + line_in[n, step]
        out_ref[:, pl.ds(n * piece, piece)] = value

    for made in [q_line, k_line, v_line, q_plane, combine] + plane_copies + line_copies:
        for copy in made.values():
            copy.wait_send()


def fused(queries, prefix_keys, prefix_values, out_weight, lengths):
    blocks = lax.axis_size("blk")
    planes = blocks // KVH
    local_rows = queries.shape[0]
    key_count = prefix_keys.shape[0]
    depth, width = out_weight.shape
    group_size = H // KVH
    tile_rows = KVH * local_rows
    row_total = planes * tile_rows
    columns = group_size * row_total
    part_cols = columns // planes
    pieces, weight_parts = 4, 8
    piece = width // pieces
    f32 = jnp.float32
    any_space = pl.BlockSpec(memory_space=pl.ANY)
    sems = pltpu.SemaphoreType.DMA
    return pl.pallas_call(
        functools.partial(fused_kernel, planes, pieces, weight_parts),
        out_shape=jax.ShapeDtypeStruct((local_rows, width), f32),
        in_specs=[any_space] * 4 + [pl.BlockSpec(memory_space=pltpu.SMEM)],
        out_specs=pl.BlockSpec(memory_space=pltpu.VMEM),
        scratch_shapes=[
            pltpu.VMEM((planes, KVH, local_rows, group_size * HD), f32),
            pltpu.VMEM((columns, HD), f32),
            pltpu.VMEM((KVH, key_count, HD), f32),
            pltpu.VMEM((KVH, key_count, HD), f32),
            pltpu.VMEM((KVH, key_count, columns), f32),
            pltpu.VMEM((depth, width), f32),
            pltpu.VMEM((depth, width), jnp.bfloat16),
            pltpu.VMEM((depth, width), jnp.bfloat16),
            pltpu.VMEM((planes, HD + 8, part_cols), f32),
            pltpu.VMEM((planes, HD + 8, part_cols), f32),
            pltpu.VMEM((pieces, planes, tile_rows, piece), f32),
            pltpu.VMEM((pieces, planes, tile_rows, piece), f32),
            pltpu.VMEM((pieces, KVH, local_rows, piece), f32),
            pltpu.VMEM((pieces, KVH, local_rows, piece), f32),
            sems((3,)),
            sems((weight_parts,)),
            sems((KVH,)),
            sems((KVH,)),
            sems((planes,)),
            sems((planes,)),
            sems((KVH,)),
            sems((KVH,)),
            sems((KVH,)),
            sems((KVH,)),
            sems((planes,)),
            sems((planes,)),
            sems((pieces, planes)),
            sems((pieces, planes)),
            sems((pieces, KVH)),
            sems((pieces, KVH)),
        ],
        compiler_params=pltpu.CompilerParams(
            collective_id=0, has_side_effects=True, vmem_limit_bytes=48 * 1024 * 1024
        ),
    )(queries, prefix_keys, prefix_values, out_weight, lengths)


def fits(mesh):
    blocks = mesh.shape["blk"]
    if blocks % KVH or (H // KVH) % (blocks // KVH):
        return False
    planes = blocks // KVH
    return planes > 1 and planes <= 8


def solution(mesh):
    in_specs = (
        P(("groups", "blk"), None),
        P(("groups", "blk"), None),
        P(("groups", "blk"), None),
        P("blk", None),
        P("groups"),
    )
    out_specs = P(("groups", "blk"), None)
    return jax.shard_map(
        fused if fits(mesh) else per_device,
        mesh=mesh,
        in_specs=in_specs,
        out_specs=out_specs,
        check_vma=False,
    )
```

```python
import functools
import math

import jax
import jax.numpy as jnp
from jax import lax
from jax.experimental import pallas as pl
from jax.experimental.pallas import tpu as pltpu
from jax.sharding import PartitionSpec as P

H = 64
KVH = 4
HD = 128
REQ_TOK = 16


HIGHEST = lax.Precision.HIGHEST
NEG_FILL = -1e30


def head_partials(query_rows, first_row, keys_split, values_split, key_pos, lengths):
    row_count = query_rows.shape[0]
    kv_count = keys_split.shape[1]
    head_count = query_rows.shape[1] // HD
    grouped = query_rows.reshape(row_count, kv_count, head_count // kv_count, HD)
    scores = jnp.einsum(
        "tgje,pge->tgjp", grouped, keys_split, precision=HIGHEST, preferred_element_type=jnp.float32
    ) * (1.0 / math.sqrt(HD))
    request_ids = (first_row + jnp.arange(row_count, dtype=jnp.int32)) // REQ_TOK
    request_table = jnp.arange(lengths.shape[0], dtype=jnp.int32)
    limits = jnp.sum(
        jnp.where(request_ids[:, None] == request_table[None, :], lengths[None, :], 0), axis=1
    )
    visible = key_pos[None, :] < limits[:, None]
    visible_four = visible[:, None, None, :]
    masked = jnp.where(visible_four, scores, NEG_FILL)
    peak_vals = jnp.max(masked, axis=3)
    weights = jnp.where(visible_four, jnp.exp(masked - peak_vals[..., None]), 0.0)
    totals = jnp.sum(weights, axis=3)
    mixed_values = jnp.einsum(
        "tgjp,pge->tgje",
        weights,
        values_split,
        precision=HIGHEST,
        preferred_element_type=jnp.float32,
    )
    return (
        mixed_values.reshape(row_count, head_count * HD),
        peak_vals.reshape(row_count, head_count),
        totals.reshape(row_count, head_count),
    )


def visit_blocks(running, shard_rows, first_row, keys_split, values_split, key_pos, lengths):
    row_count = shard_rows.shape[0]
    step_rows = 32

    def advance(step_id, current):
        row_begin = first_row + step_id * step_rows
        rows_now = lax.dynamic_slice_in_dim(shard_rows, step_id * step_rows, step_rows, 0)
        parts_now = head_partials(rows_now, row_begin, keys_split, values_split, key_pos, lengths)
        return tuple(
            (
                lax.dynamic_update_slice_in_dim(whole_arr, piece_now, row_begin, 0)
                for whole_arr, piece_now in zip(current, parts_now)
            )
        )

    return lax.fori_loop(0, row_count // step_rows, advance, running)


def per_device(queries, prefix_keys, prefix_values, out_weight, lengths):
    blocks = lax.axis_size("blk")
    position = lax.axis_index("blk")
    local_rows = queries.shape[0]
    total_rows = local_rows * blocks
    feature_count = H * HD
    key_count = prefix_keys.shape[0]
    group_size = H // KVH
    sub_count = blocks // KVH
    sub_len = key_count // sub_count
    key_send = (
        prefix_keys.reshape(sub_count, sub_len, KVH, HD)
        .transpose(0, 2, 1, 3)
        .reshape(blocks, sub_len, HD)
    )
    value_send = (
        prefix_values.reshape(sub_count, sub_len, KVH, HD)
        .transpose(0, 2, 1, 3)
        .reshape(blocks, sub_len, HD)
    )
    held_keys, held_values = (
        lax.all_to_all(key_send, "blk", split_axis=0, concat_axis=0, tiled=True),
        lax.all_to_all(value_send, "blk", split_axis=0, concat_axis=0, tiled=True),
    )
    sub_index = position // KVH
    source_ids = jnp.arange(blocks, dtype=jnp.int32)
    held_pos = (
        source_ids[:, None] * key_count
        + sub_index * sub_len
        + jnp.arange(sub_len, dtype=jnp.int32)[None, :]
    ).reshape(blocks * sub_len)
    held_keys = held_keys.reshape(blocks * sub_len, 1, HD)
    held_values = held_values.reshape(blocks * sub_len, 1, HD)
    query_heads = queries.reshape(local_rows, KVH, group_size * HD).transpose(1, 0, 2)
    query_send = jnp.broadcast_to(
        query_heads[None], (sub_count, KVH, local_rows, group_size * HD)
    ).reshape(blocks, local_rows, group_size * HD)
    query_held = lax.all_to_all(query_send, "blk", split_axis=0, concat_axis=0, tiled=True).reshape(
        total_rows, group_size * HD
    )
    empty_heads = (
        jnp.zeros((total_rows, group_size * HD), jnp.float32),
        jnp.zeros((total_rows, group_size), jnp.float32),
        jnp.zeros((total_rows, group_size), jnp.float32),
    )
    part_sums, part_peaks, part_totals = visit_blocks(
        empty_heads, query_held, 0, held_keys, held_values, held_pos, lengths
    )
    back_sums, back_peaks, back_totals = (
        lax.all_to_all(part_sums, "blk", split_axis=0, concat_axis=0, tiled=True),
        lax.all_to_all(part_peaks, "blk", split_axis=0, concat_axis=0, tiled=True),
        lax.all_to_all(part_totals, "blk", split_axis=0, concat_axis=0, tiled=True),
    )
    sums_split = back_sums.reshape(sub_count, KVH, local_rows, group_size, HD)
    peaks_split = back_peaks.reshape(sub_count, KVH, local_rows, group_size)
    overall = jnp.max(peaks_split, axis=0)
    factor = jnp.exp(peaks_split - overall[None])
    numerator = jnp.sum(sums_split * factor[..., None], axis=0)
    denominator = jnp.sum(
        back_totals.reshape(sub_count, KVH, local_rows, group_size) * factor, axis=0
    )
    attended = (
        (numerator / denominator[..., None])
        .transpose(1, 0, 2, 3)
        .reshape(local_rows, feature_count)
    )
    feature_rows = lax.all_to_all(attended, "blk", split_axis=1, concat_axis=0, tiled=True)
    return lax.psum_scatter(
        jnp.dot(feature_rows, out_weight, precision=HIGHEST, preferred_element_type=jnp.float32),
        "blk",
        scatter_dimension=0,
        tiled=True,
    )

def split_two(values):
    high = values.astype(jnp.bfloat16)
    return high, (values - high.astype(jnp.float32)).astype(jnp.bfloat16)


def fused_kernel(
    planes,
    pieces,
    weight_parts,
    q_hbm,
    k_hbm,
    v_hbm,
    w_hbm,
    len_hbm,
    out_ref,
    len_ref,
    q_all,
    q_rows,
    k_all,
    v_all,
    scores,
    w_full,
    w_high,
    w_low,
    part_out,
    part_in,
    plane_out,
    plane_in,
    line_out,
    line_in,
    own_sem,
    w_sem,
    qz_send,
    qz_recv,
    qp_send,
    qp_recv,
    k_send,
    k_recv,
    v_send,
    v_recv,
    c_send,
    c_recv,
    r_send,
    r_recv,
    l_send,
    l_recv,
):
    me = lax.axis_index("blk")
    line = lax.div(me, planes)
    spot = lax.rem(me, planes)
    group_size = H // KVH
    group_width = group_size * HD
    local_rows = q_hbm.shape[0]
    key_count = k_hbm.shape[0]
    tile_rows = KVH * local_rows
    row_total = planes * tile_rows
    own_heads = group_size // planes
    width = w_hbm.shape[1]

    def remote(src, dst, send, recv, target):
        return pltpu.make_async_remote_copy(
            src_ref=src,
            dst_ref=dst,
            send_sem=send,
            recv_sem=recv,
            device_id={"blk": target},
            device_id_type=pl.DeviceIdType.MESH,
        )

    def line_peer(step):
        return lax.rem(line + step, KVH)

    def plane_peer(step):
        return lax.rem(spot + step, planes)

    def head_cols(ref, head, size):
        return ref.at[:, pl.ds(pl.multiple_of(head * size, size), size)]

    line_steps = [2, 1, 3] if KVH == 4 else list(range(1, KVH))
    plane_steps = list(range(1, planes))

    own = [
        pltpu.make_async_copy(head_cols(q_hbm, line, group_width), q_all.at[spot, 0], own_sem.at[0]),
        pltpu.make_async_copy(head_cols(k_hbm, line, HD), k_all.at[0], own_sem.at[1]),
        pltpu.make_async_copy(head_cols(v_hbm, line, HD), v_all.at[0], own_sem.at[2]),
        pltpu.make_async_copy(len_hbm, len_ref, own_sem.at[3]),
    ]
    for copy in own:
        copy.start()
    w_step = w_hbm.shape[0] // weight_parts
    w_copies = [
        pltpu.make_async_copy(
            w_hbm.at[pl.ds(n * w_step, w_step)], w_full.at[pl.ds(n * w_step, w_step)], w_sem.at[n]
        )
        for n in range(weight_parts)
    ]
    for copy in w_copies:
        copy.start()

    barrier = pltpu.get_barrier_semaphore()
    for step in line_steps:
        pl.semaphore_signal(
            barrier,
            inc=1,
            device_id={"blk": line_peer(step) * planes + spot},
            device_id_type=pl.DeviceIdType.MESH,
        )
    for step in plane_steps:
        pl.semaphore_signal(
            barrier,
            inc=1,
            device_id={"blk": line * planes + plane_peer(step)},
            device_id_type=pl.DeviceIdType.MESH,
        )
    pl.semaphore_wait(barrier, len(line_steps) + len(plane_steps))

    q_line, k_line, v_line = {}, {}, {}
    for step in line_steps:
        head = line_peer(step)
        q_line[step] = remote(
            head_cols(q_hbm, head, group_width),
            q_all.at[spot, step],
            qz_send.at[step],
            qz_recv.at[step],
            head * planes + spot,
        )
        q_line[step].start()
    for source, target, send, recv, made in (
        (k_hbm, k_all, k_send, k_recv, k_line),
        (v_hbm, v_all, v_send, v_recv, v_line),
    ):
        for step in line_steps:
            head = line_peer(step)
            made[step] = remote(
                head_cols(source, head, HD),
                target.at[step],
                send.at[step],
                recv.at[step],
                head * planes + spot,
            )
            made[step].start()

    split_rows, split_cols = 16, width // 2

    def split_part(part):
        w_copies[part].wait()

        def body(at, carry):
            rows = pl.ds(pl.multiple_of(part * w_step + at * split_rows, split_rows), split_rows)
            for half in range(width // split_cols):
                cols = pl.ds(half * split_cols, split_cols)
                high, low = split_two(w_full[rows, cols])
                w_high[rows, cols] = high
                w_low[rows, cols] = low
            return carry

        lax.fori_loop(0, w_step // split_rows, body, 0)

    early = weight_parts // 2
    for part in range(early):
        split_part(part)

    own[0].wait()
    for step in line_steps:
        q_line[step].wait_recv()
    q_plane = {}
    for step in plane_steps:
        q_plane[step] = remote(
            q_all.at[spot],
            q_all.at[spot],
            qp_send.at[step],
            qp_recv.at[step],
            line * planes + plane_peer(step),
        )
        q_plane[step].start()
    for part in range(early, weight_parts):
        split_part(part)
    for step in plane_steps:
        q_plane[step].wait_recv()

    for place in range(planes):
        for step in range(KVH):
            first = place * tile_rows + step * local_rows
            for head in range(group_size):
                q_rows[pl.ds(head * row_total + first, local_rows), :] = q_all[
                    place, step, :, pl.ds(head * HD, HD)
                ]
    query = q_rows[...]

    columns = group_size * row_total
    lane = lax.broadcasted_iota(jnp.int32, (1, columns), 1) % row_total
    lane_line = (line - (lane % tile_rows) // local_rows + KVH) % KVH
    token = (lane_line * planes + lane // tile_rows) * local_rows + lane % local_rows
    request = token // REQ_TOK
    own[3].wait()
    limits = jnp.zeros((1, columns), jnp.int32)
    for n in range(len_ref.shape[0]):
        limits = jnp.where(request == n, len_ref[n], limits)

    def key_place(step):
        source = lax.rem(line - step + KVH, KVH) * planes + spot
        return source * key_count + lax.broadcasted_iota(jnp.int32, (key_count, 1), 0)

    scale = 1.0 / math.sqrt(HD)
    peak = None
    for step in [0] + line_steps:
        if step == 0:
            own[1].wait()
        else:
            k_line[step].wait_recv()
        block = (
            lax.dot_general(
                k_all[step],
                query,
                (((1,), (1,)), ((), ())),
                precision=HIGHEST,
                preferred_element_type=jnp.float32,
            )
            * scale
        )
        block = jnp.where(key_place(step) < limits, block, NEG_FILL)
        scores[step] = block
        top = jnp.max(block, axis=0, keepdims=True)
        peak = top if peak is None else jnp.maximum(peak, top)
    total = jnp.zeros((1, columns), jnp.float32)
    for step in range(KVH):
        weights = jnp.where(key_place(step) < limits, jnp.exp(scores[step] - peak), 0.0)
        total = total + jnp.sum(weights, axis=0, keepdims=True)
        scores[step] = weights
    sums = jnp.zeros((HD, columns), jnp.float32)
    for step in [0] + line_steps:
        if step == 0:
            own[2].wait()
        else:
            v_line[step].wait_recv()
        sums = sums + lax.dot_general(
            v_all[step],
            scores[step],
            (((0,), (0,)), ((), ())),
            precision=HIGHEST,
            preferred_element_type=jnp.float32,
        )

    part_cols = own_heads * row_total
    for place in range(planes):
        cols = slice(place * part_cols, (place + 1) * part_cols)
        part_out[place, pl.ds(0, HD), :] = sums[:, cols]
        part_out[place, pl.ds(HD, 1), :] = peak[:, cols]
        part_out[place, pl.ds(HD + 1, 1), :] = total[:, cols]
    combine = {}
    for step in plane_steps:
        place = plane_peer(step)
        combine[step] = remote(
            part_out.at[place],
            part_in.at[step],
            c_send.at[step],
            c_recv.at[step],
            line * planes + place,
        )
        combine[step].start()
    for step in plane_steps:
        combine[step].wait_recv()
    peaks = [part_out[spot, pl.ds(HD, 1), :]] + [part_in[n, pl.ds(HD, 1), :] for n in plane_steps]
    totals = [part_out[spot, pl.ds(HD + 1, 1), :]] + [
        part_in[n, pl.ds(HD + 1, 1), :] for n in plane_steps
    ]
    overall = functools.reduce(jnp.maximum, peaks)
    factors = [jnp.exp(value - overall) for value in peaks]
    denominator = sum(value * factor for value, factor in zip(totals, factors))
    numerator = part_out[spot, pl.ds(0, HD), :] * factors[0]
    for step in plane_steps:
        numerator = numerator + part_in[step, pl.ds(0, HD), :] * factors[step]
    attended = (numerator / denominator).T
    features = jnp.concatenate(
        [attended[n * row_total : (n + 1) * row_total] for n in range(own_heads)], axis=1
    )
    high, low = split_two(features)
    both = jnp.concatenate([high, low], axis=0)

    piece = width // pieces
    plane_copies = []
    for n in range(pieces):
        cols = pl.ds(n * piece, piece)
        first = jnp.dot(both, w_high[:, cols], preferred_element_type=jnp.float32)
        second = jnp.dot(high, w_low[:, cols], preferred_element_type=jnp.float32)
        mixed = first[:row_total] + first[row_total:] + second
        for place in range(planes):
            plane_out[n, place] = mixed[place * tile_rows : (place + 1) * tile_rows]
        made = {}
        for step in plane_steps:
            place = plane_peer(step)
            made[step] = remote(
                plane_out.at[n, place],
                plane_in.at[n, step],
                r_send.at[n, step],
                r_recv.at[n, step],
                line * planes + place,
            )
            made[step].start()
        plane_copies.append(made)

    line_copies = []
    for n in range(pieces):
        value = plane_out[n, spot]
        for step in plane_steps:
            plane_copies[n][step].wait_recv()
            value = value + plane_in[n, step]
        for step in range(KVH):
            line_out[n, step] = value[step * local_rows : (step + 1) * local_rows]
        made = {}
        for step in line_steps:
            target = lax.rem(line - step + KVH, KVH) * planes + spot
            made[step] = remote(
                line_out.at[n, step],
                line_in.at[n, step],
                l_send.at[n, step],
                l_recv.at[n, step],
                target,
            )
            made[step].start()
        line_copies.append(made)
    for n in range(pieces):
        value = line_out[n, 0]
        for step in line_steps:
            line_copies[n][step].wait_recv()
            value = value + line_in[n, step]
        out_ref[:, pl.ds(n * piece, piece)] = value

    for made in [q_line, k_line, v_line, q_plane, combine] + plane_copies + line_copies:
        for copy in made.values():
            copy.wait_send()


def fused(queries, prefix_keys, prefix_values, out_weight, lengths):
    blocks = lax.axis_size("blk")
    planes = blocks // KVH
    local_rows = queries.shape[0]
    key_count = prefix_keys.shape[0]
    depth, width = out_weight.shape
    group_size = H // KVH
    tile_rows = KVH * local_rows
    row_total = planes * tile_rows
    columns = group_size * row_total
    part_cols = columns // planes
    pieces, weight_parts = 4, 8
    piece = width // pieces
    f32 = jnp.float32
    any_space = pl.BlockSpec(memory_space=pltpu.HBM)
    sems = pltpu.SemaphoreType.DMA
    return pl.pallas_call(
        functools.partial(fused_kernel, planes, pieces, weight_parts),
        out_shape=jax.ShapeDtypeStruct((local_rows, width), f32),
        in_specs=[any_space] * 5,
        out_specs=pl.BlockSpec(memory_space=pltpu.VMEM),
        scratch_shapes=[
            pltpu.SMEM(lengths.shape, lengths.dtype),
            pltpu.VMEM((planes, KVH, local_rows, group_size * HD), f32),
            pltpu.VMEM((columns, HD), f32),
            pltpu.VMEM((KVH, key_count, HD), f32),
            pltpu.VMEM((KVH, key_count, HD), f32),
            pltpu.VMEM((KVH, key_count, columns), f32),
            pltpu.VMEM((depth, width), f32),
            pltpu.VMEM((depth, width), jnp.bfloat16),
            pltpu.VMEM((depth, width), jnp.bfloat16),
            pltpu.VMEM((planes, HD + 8, part_cols), f32),
            pltpu.VMEM((planes, HD + 8, part_cols), f32),
            pltpu.VMEM((pieces, planes, tile_rows, piece), f32),
            pltpu.VMEM((pieces, planes, tile_rows, piece), f32),
            pltpu.VMEM((pieces, KVH, local_rows, piece), f32),
            pltpu.VMEM((pieces, KVH, local_rows, piece), f32),
            sems((4,)),
            sems((weight_parts,)),
            sems((KVH,)),
            sems((KVH,)),
            sems((planes,)),
            sems((planes,)),
            sems((KVH,)),
            sems((KVH,)),
            sems((KVH,)),
            sems((KVH,)),
            sems((planes,)),
            sems((planes,)),
            sems((pieces, planes)),
            sems((pieces, planes)),
            sems((pieces, KVH)),
            sems((pieces, KVH)),
        ],
        compiler_params=pltpu.CompilerParams(
            collective_id=0, has_side_effects=True, vmem_limit_bytes=64 * 1024 * 1024
        ),
    )(queries, prefix_keys, prefix_values, out_weight, lengths)


def fits(mesh):
    blocks = mesh.shape["blk"]
    if blocks % KVH or (H // KVH) % (blocks // KVH):
        return False
    planes = blocks // KVH
    return planes > 1 and planes <= 8


def solution(mesh):
    in_specs = (
        P(("groups", "blk"), None),
        P(("groups", "blk"), None),
        P(("groups", "blk"), None),
        P("blk", None),
        P("groups"),
    )
    out_specs = P(("groups", "blk"), None)
    return jax.shard_map(
        fused if fits(mesh) else per_device,
        mesh=mesh,
        in_specs=in_specs,
        out_specs=out_specs,
        check_vma=False,
    )
```

```python
import functools
import math

import jax
import jax.numpy as jnp
from jax import lax
from jax.experimental import pallas as pl
from jax.experimental.pallas import tpu as pltpu
from jax.sharding import PartitionSpec as P

H = 64
KVH = 4
HD = 128
REQ_TOK = 16
PAIR = 2


HIGHEST = lax.Precision.HIGHEST
NEG_FILL = -1e30


def head_partials(query_rows, first_row, keys_split, values_split, key_pos, lengths):
    row_count = query_rows.shape[0]
    kv_count = keys_split.shape[1]
    head_count = query_rows.shape[1] // HD
    grouped = query_rows.reshape(row_count, kv_count, head_count // kv_count, HD)
    scores = jnp.einsum(
        "tgje,pge->tgjp", grouped, keys_split, precision=HIGHEST, preferred_element_type=jnp.float32
    ) * (1.0 / math.sqrt(HD))
    request_ids = (first_row + jnp.arange(row_count, dtype=jnp.int32)) // REQ_TOK
    request_table = jnp.arange(lengths.shape[0], dtype=jnp.int32)
    limits = jnp.sum(
        jnp.where(request_ids[:, None] == request_table[None, :], lengths[None, :], 0), axis=1
    )
    visible = key_pos[None, :] < limits[:, None]
    visible_four = visible[:, None, None, :]
    masked = jnp.where(visible_four, scores, NEG_FILL)
    peak_vals = jnp.max(masked, axis=3)
    weights = jnp.where(visible_four, jnp.exp(masked - peak_vals[..., None]), 0.0)
    totals = jnp.sum(weights, axis=3)
    mixed_values = jnp.einsum(
        "tgjp,pge->tgje",
        weights,
        values_split,
        precision=HIGHEST,
        preferred_element_type=jnp.float32,
    )
    return (
        mixed_values.reshape(row_count, head_count * HD),
        peak_vals.reshape(row_count, head_count),
        totals.reshape(row_count, head_count),
    )


def visit_blocks(running, shard_rows, first_row, keys_split, values_split, key_pos, lengths):
    row_count = shard_rows.shape[0]
    step_rows = 32

    def advance(step_id, current):
        row_begin = first_row + step_id * step_rows
        rows_now = lax.dynamic_slice_in_dim(shard_rows, step_id * step_rows, step_rows, 0)
        parts_now = head_partials(rows_now, row_begin, keys_split, values_split, key_pos, lengths)
        return tuple(
            (
                lax.dynamic_update_slice_in_dim(whole_arr, piece_now, row_begin, 0)
                for whole_arr, piece_now in zip(current, parts_now)
            )
        )

    return lax.fori_loop(0, row_count // step_rows, advance, running)


def per_device(queries, prefix_keys, prefix_values, out_weight, lengths):
    blocks = lax.axis_size("blk")
    position = lax.axis_index("blk")
    local_rows = queries.shape[0]
    total_rows = local_rows * blocks
    feature_count = H * HD
    key_count = prefix_keys.shape[0]
    group_size = H // KVH
    sub_count = blocks // KVH
    sub_len = key_count // sub_count
    key_send = (
        prefix_keys.reshape(sub_count, sub_len, KVH, HD)
        .transpose(0, 2, 1, 3)
        .reshape(blocks, sub_len, HD)
    )
    value_send = (
        prefix_values.reshape(sub_count, sub_len, KVH, HD)
        .transpose(0, 2, 1, 3)
        .reshape(blocks, sub_len, HD)
    )
    held_keys, held_values = (
        lax.all_to_all(key_send, "blk", split_axis=0, concat_axis=0, tiled=True),
        lax.all_to_all(value_send, "blk", split_axis=0, concat_axis=0, tiled=True),
    )
    sub_index = position // KVH
    source_ids = jnp.arange(blocks, dtype=jnp.int32)
    held_pos = (
        source_ids[:, None] * key_count
        + sub_index * sub_len
        + jnp.arange(sub_len, dtype=jnp.int32)[None, :]
    ).reshape(blocks * sub_len)
    held_keys = held_keys.reshape(blocks * sub_len, 1, HD)
    held_values = held_values.reshape(blocks * sub_len, 1, HD)
    query_heads = queries.reshape(local_rows, KVH, group_size * HD).transpose(1, 0, 2)
    query_send = jnp.broadcast_to(
        query_heads[None], (sub_count, KVH, local_rows, group_size * HD)
    ).reshape(blocks, local_rows, group_size * HD)
    query_held = lax.all_to_all(query_send, "blk", split_axis=0, concat_axis=0, tiled=True).reshape(
        total_rows, group_size * HD
    )
    empty_heads = (
        jnp.zeros((total_rows, group_size * HD), jnp.float32),
        jnp.zeros((total_rows, group_size), jnp.float32),
        jnp.zeros((total_rows, group_size), jnp.float32),
    )
    part_sums, part_peaks, part_totals = visit_blocks(
        empty_heads, query_held, 0, held_keys, held_values, held_pos, lengths
    )
    back_sums, back_peaks, back_totals = (
        lax.all_to_all(part_sums, "blk", split_axis=0, concat_axis=0, tiled=True),
        lax.all_to_all(part_peaks, "blk", split_axis=0, concat_axis=0, tiled=True),
        lax.all_to_all(part_totals, "blk", split_axis=0, concat_axis=0, tiled=True),
    )
    sums_split = back_sums.reshape(sub_count, KVH, local_rows, group_size, HD)
    peaks_split = back_peaks.reshape(sub_count, KVH, local_rows, group_size)
    overall = jnp.max(peaks_split, axis=0)
    factor = jnp.exp(peaks_split - overall[None])
    numerator = jnp.sum(sums_split * factor[..., None], axis=0)
    denominator = jnp.sum(
        back_totals.reshape(sub_count, KVH, local_rows, group_size) * factor, axis=0
    )
    attended = (
        (numerator / denominator[..., None])
        .transpose(1, 0, 2, 3)
        .reshape(local_rows, feature_count)
    )
    feature_rows = lax.all_to_all(attended, "blk", split_axis=1, concat_axis=0, tiled=True)
    return lax.psum_scatter(
        jnp.dot(feature_rows, out_weight, precision=HIGHEST, preferred_element_type=jnp.float32),
        "blk",
        scatter_dimension=0,
        tiled=True,
    )

def split_two(values):
    high = values.astype(jnp.bfloat16)
    return high, (values - high.astype(jnp.float32)).astype(jnp.bfloat16)


def fused_kernel(
    planes,
    pieces,
    weight_parts,
    q_hbm,
    k_hbm,
    v_hbm,
    w_hbm,
    len_hbm,
    out_ref,
    len_ref,
    q_all,
    q_rows,
    k_all,
    v_all,
    scores,
    w_full,
    w_high,
    w_low,
    part_out,
    part_in,
    plane_out,
    pair_in,
    pair_out,
    plane_in,
    line_out,
    line_in,
    own_sem,
    w_sem,
    qz_send,
    qz_recv,
    qp_send,
    qp_recv,
    k_send,
    k_recv,
    v_send,
    v_recv,
    c_send,
    c_recv,
    p_send,
    p_recv,
    r_send,
    r_recv,
    l_send,
    l_recv,
):
    me = lax.axis_index("blk")
    line = lax.div(me, planes)
    spot = lax.rem(me, planes)
    side, core = lax.div(spot, PAIR), lax.rem(spot, PAIR)
    sides = planes // PAIR
    group_size = H // KVH
    group_width = group_size * HD
    local_rows = q_hbm.shape[0]
    key_count = k_hbm.shape[0]
    tile_rows = KVH * local_rows
    row_total = planes * tile_rows
    own_heads = group_size // planes
    width = w_hbm.shape[1]

    def remote(src, dst, send, recv, target):
        return pltpu.make_async_remote_copy(
            src_ref=src,
            dst_ref=dst,
            send_sem=send,
            recv_sem=recv,
            device_id={"blk": target},
            device_id_type=pl.DeviceIdType.MESH,
        )

    def line_peer(step):
        return lax.rem(line + step, KVH)

    def plane_peer(step):
        return lax.rem(spot + step, planes)

    def head_cols(ref, head, size):
        return ref.at[:, pl.ds(pl.multiple_of(head * size, size), size)]

    line_steps = [2, 1, 3] if KVH == 4 else list(range(1, KVH))
    plane_steps = list(range(1, planes))

    own = [
        pltpu.make_async_copy(head_cols(q_hbm, line, group_width), q_all.at[spot, 0], own_sem.at[0]),
        pltpu.make_async_copy(head_cols(k_hbm, line, HD), k_all.at[0], own_sem.at[1]),
        pltpu.make_async_copy(head_cols(v_hbm, line, HD), v_all.at[0], own_sem.at[2]),
        pltpu.make_async_copy(len_hbm, len_ref, own_sem.at[3]),
    ]
    for copy in own:
        copy.start()
    w_step = w_hbm.shape[0] // weight_parts
    w_copies = [
        pltpu.make_async_copy(
            w_hbm.at[pl.ds(n * w_step, w_step)], w_full.at[pl.ds(n * w_step, w_step)], w_sem.at[n]
        )
        for n in range(weight_parts)
    ]
    for copy in w_copies:
        copy.start()

    barrier = pltpu.get_barrier_semaphore()
    for step in line_steps:
        pl.semaphore_signal(
            barrier,
            inc=1,
            device_id={"blk": line_peer(step) * planes + spot},
            device_id_type=pl.DeviceIdType.MESH,
        )
    for step in plane_steps:
        pl.semaphore_signal(
            barrier,
            inc=1,
            device_id={"blk": line * planes + plane_peer(step)},
            device_id_type=pl.DeviceIdType.MESH,
        )
    pl.semaphore_wait(barrier, len(line_steps) + len(plane_steps))

    q_line, k_line, v_line = {}, {}, {}
    for step in line_steps:
        head = line_peer(step)
        q_line[step] = remote(
            head_cols(q_hbm, head, group_width),
            q_all.at[spot, step],
            qz_send.at[step],
            qz_recv.at[step],
            head * planes + spot,
        )
        q_line[step].start()
    for source, target, send, recv, made in (
        (k_hbm, k_all, k_send, k_recv, k_line),
        (v_hbm, v_all, v_send, v_recv, v_line),
    ):
        for step in line_steps:
            head = line_peer(step)
            made[step] = remote(
                head_cols(source, head, HD),
                target.at[step],
                send.at[step],
                recv.at[step],
                head * planes + spot,
            )
            made[step].start()

    split_rows, split_cols = 16, width // 2

    def split_part(part):
        w_copies[part].wait()

        def body(at, carry):
            rows = pl.ds(pl.multiple_of(part * w_step + at * split_rows, split_rows), split_rows)
            for half in range(width // split_cols):
                cols = pl.ds(half * split_cols, split_cols)
                high, low = split_two(w_full[rows, cols])
                w_high[rows, cols] = high
                w_low[rows, cols] = low
            return carry

        lax.fori_loop(0, w_step // split_rows, body, 0)

    early = weight_parts // 2
    for part in range(early):
        split_part(part)

    own[0].wait()
    for step in line_steps:
        q_line[step].wait_recv()
    q_plane = {}
    for step in plane_steps:
        q_plane[step] = remote(
            q_all.at[spot],
            q_all.at[spot],
            qp_send.at[step],
            qp_recv.at[step],
            line * planes + plane_peer(step),
        )
        q_plane[step].start()
    for part in range(early, weight_parts):
        split_part(part)
    for step in plane_steps:
        q_plane[step].wait_recv()

    for place in range(planes):
        for step in range(KVH):
            first = place * tile_rows + step * local_rows
            for head in range(group_size):
                q_rows[pl.ds(head * row_total + first, local_rows), :] = q_all[
                    place, step, :, pl.ds(head * HD, HD)
                ]
    query = q_rows[...]

    columns = group_size * row_total
    lane = lax.broadcasted_iota(jnp.int32, (1, columns), 1) % row_total
    lane_line = (line - (lane % tile_rows) // local_rows + KVH) % KVH
    token = (lane_line * planes + lane // tile_rows) * local_rows + lane % local_rows
    request = token // REQ_TOK
    own[3].wait()
    limits = jnp.zeros((1, columns), jnp.int32)
    for n in range(len_ref.shape[0]):
        limits = jnp.where(request == n, len_ref[n], limits)

    def key_place(step):
        source = lax.rem(line - step + KVH, KVH) * planes + spot
        return source * key_count + lax.broadcasted_iota(jnp.int32, (key_count, 1), 0)

    scale = 1.0 / math.sqrt(HD)
    peak = None
    for step in [0] + line_steps:
        if step == 0:
            own[1].wait()
        else:
            k_line[step].wait_recv()
        block = (
            lax.dot_general(
                k_all[step],
                query,
                (((1,), (1,)), ((), ())),
                precision=HIGHEST,
                preferred_element_type=jnp.float32,
            )
            * scale
        )
        block = jnp.where(key_place(step) < limits, block, NEG_FILL)
        scores[step] = block
        top = jnp.max(block, axis=0, keepdims=True)
        peak = top if peak is None else jnp.maximum(peak, top)
    total = jnp.zeros((1, columns), jnp.float32)
    for step in range(KVH):
        weights = jnp.where(key_place(step) < limits, jnp.exp(scores[step] - peak), 0.0)
        total = total + jnp.sum(weights, axis=0, keepdims=True)
        scores[step] = weights
    sums = jnp.zeros((HD, columns), jnp.float32)
    for step in [0] + line_steps:
        if step == 0:
            own[2].wait()
        else:
            v_line[step].wait_recv()
        sums = sums + lax.dot_general(
            v_all[step],
            scores[step],
            (((0,), (0,)), ((), ())),
            precision=HIGHEST,
            preferred_element_type=jnp.float32,
        )

    part_cols = own_heads * row_total
    for place in range(planes):
        cols = slice(place * part_cols, (place + 1) * part_cols)
        part_out[place, pl.ds(0, HD), :] = sums[:, cols]
        part_out[place, pl.ds(HD, 1), :] = peak[:, cols]
        part_out[place, pl.ds(HD + 1, 1), :] = total[:, cols]
    combine = {}
    for step in plane_steps:
        place = plane_peer(step)
        combine[step] = remote(
            part_out.at[place],
            part_in.at[step],
            c_send.at[step],
            c_recv.at[step],
            line * planes + place,
        )
        combine[step].start()
    for step in plane_steps:
        combine[step].wait_recv()
    peaks = [part_out[spot, pl.ds(HD, 1), :]] + [part_in[n, pl.ds(HD, 1), :] for n in plane_steps]
    totals = [part_out[spot, pl.ds(HD + 1, 1), :]] + [
        part_in[n, pl.ds(HD + 1, 1), :] for n in plane_steps
    ]
    overall = functools.reduce(jnp.maximum, peaks)
    factors = [jnp.exp(value - overall) for value in peaks]
    denominator = sum(value * factor for value, factor in zip(totals, factors))
    numerator = part_out[spot, pl.ds(0, HD), :] * factors[0]
    for step in plane_steps:
        numerator = numerator + part_in[step, pl.ds(0, HD), :] * factors[step]
    attended = (numerator / denominator).T
    features = jnp.concatenate(
        [attended[n * row_total : (n + 1) * row_total] for n in range(own_heads)], axis=1
    )
    high, low = split_two(features)
    both = jnp.concatenate([high, low], axis=0)

    piece = width // pieces
    pair_copies, plane_copies, line_copies = [], [], []

    def project(n):
        cols = pl.ds(n * piece, piece)
        first = jnp.dot(both, w_high[:, cols], preferred_element_type=jnp.float32)
        second = jnp.dot(high, w_low[:, cols], preferred_element_type=jnp.float32)
        mixed = first[:row_total] + first[row_total:] + second
        for place in range(planes):
            plane_out[n, place % PAIR, place // PAIR] = mixed[
                place * tile_rows : (place + 1) * tile_rows
            ]
        made = {}
        for step in range(1, PAIR):
            other = lax.rem(core + step, PAIR)
            made[step] = remote(
                plane_out.at[n, other],
                pair_in.at[n, step],
                p_send.at[n, step],
                p_recv.at[n, step],
                line * planes + side * PAIR + other,
            )
            made[step].start()
        pair_copies.append(made)

    def add_pair(n):
        value = plane_out[n, core]
        for step in range(1, PAIR):
            pair_copies[n][step].wait_recv()
            value = value + pair_in[n, step]
        pair_out[n] = value
        made = {}
        for step in range(1, sides):
            other = lax.rem(side + step, sides)
            made[step] = remote(
                pair_out.at[n, other],
                plane_in.at[n, step],
                r_send.at[n, step],
                r_recv.at[n, step],
                line * planes + other * PAIR + core,
            )
            made[step].start()
        plane_copies.append(made)

    ahead = min(2, pieces)
    for n in range(pieces + ahead):
        if n < pieces:
            project(n)
        if n >= ahead:
            add_pair(n - ahead)

    for n in range(pieces):
        value = pair_out[n, side]
        for step in range(1, sides):
            plane_copies[n][step].wait_recv()
            value = value + plane_in[n, step]
        for step in range(KVH):
            line_out[n, step] = value[step * local_rows : (step + 1) * local_rows]
        made = {}
        for step in line_steps:
            target = lax.rem(line - step + KVH, KVH) * planes + spot
            made[step] = remote(
                line_out.at[n, step],
                line_in.at[n, step],
                l_send.at[n, step],
                l_recv.at[n, step],
                target,
            )
            made[step].start()
        line_copies.append(made)
    for n in range(pieces):
        value = line_out[n, 0]
        for step in line_steps:
            line_copies[n][step].wait_recv()
            value = value + line_in[n, step]
        out_ref[:, pl.ds(n * piece, piece)] = value

    for made in [q_line, k_line, v_line, q_plane, combine] + pair_copies + plane_copies + line_copies:
        for copy in made.values():
            copy.wait_send()


def fused(queries, prefix_keys, prefix_values, out_weight, lengths):
    blocks = lax.axis_size("blk")
    planes = blocks // KVH
    sides = planes // PAIR
    local_rows = queries.shape[0]
    key_count = prefix_keys.shape[0]
    depth, width = out_weight.shape
    group_size = H // KVH
    tile_rows = KVH * local_rows
    row_total = planes * tile_rows
    columns = group_size * row_total
    part_cols = columns // planes
    pieces, weight_parts = 4, 8
    piece = width // pieces
    f32 = jnp.float32
    any_space = pl.BlockSpec(memory_space=pltpu.HBM)
    sems = pltpu.SemaphoreType.DMA
    return pl.pallas_call(
        functools.partial(fused_kernel, planes, pieces, weight_parts),
        out_shape=jax.ShapeDtypeStruct((local_rows, width), f32),
        in_specs=[any_space] * 5,
        out_specs=pl.BlockSpec(memory_space=pltpu.VMEM),
        scratch_shapes=[
            pltpu.SMEM(lengths.shape, lengths.dtype),
            pltpu.VMEM((planes, KVH, local_rows, group_size * HD), f32),
            pltpu.VMEM((columns, HD), f32),
            pltpu.VMEM((KVH, key_count, HD), f32),
            pltpu.VMEM((KVH, key_count, HD), f32),
            pltpu.VMEM((KVH, key_count, columns), f32),
            pltpu.VMEM((depth, width), f32),
            pltpu.VMEM((depth, width), jnp.bfloat16),
            pltpu.VMEM((depth, width), jnp.bfloat16),
            pltpu.VMEM((planes, HD + 8, part_cols), f32),
            pltpu.VMEM((planes, HD + 8, part_cols), f32),
            pltpu.VMEM((pieces, PAIR, sides, tile_rows, piece), f32),
            pltpu.VMEM((pieces, PAIR, sides, tile_rows, piece), f32),
            pltpu.VMEM((pieces, sides, tile_rows, piece), f32),
            pltpu.VMEM((pieces, sides, tile_rows, piece), f32),
            pltpu.VMEM((pieces, KVH, local_rows, piece), f32),
            pltpu.VMEM((pieces, KVH, local_rows, piece), f32),
            sems((4,)),
            sems((weight_parts,)),
            sems((KVH,)),
            sems((KVH,)),
            sems((planes,)),
            sems((planes,)),
            sems((KVH,)),
            sems((KVH,)),
            sems((KVH,)),
            sems((KVH,)),
            sems((planes,)),
            sems((planes,)),
            sems((pieces, PAIR)),
            sems((pieces, PAIR)),
            sems((pieces, sides)),
            sems((pieces, sides)),
            sems((pieces, KVH)),
            sems((pieces, KVH)),
        ],
        compiler_params=pltpu.CompilerParams(
            collective_id=0, has_side_effects=True, vmem_limit_bytes=64 * 1024 * 1024
        ),
    )(queries, prefix_keys, prefix_values, out_weight, lengths)


def fits(mesh):
    blocks = mesh.shape["blk"]
    if blocks % KVH or (H // KVH) % (blocks // KVH):
        return False
    planes = blocks // KVH
    return planes % PAIR == 0 and planes <= 8


def solution(mesh):
    in_specs = (
        P(("groups", "blk"), None),
        P(("groups", "blk"), None),
        P(("groups", "blk"), None),
        P("blk", None),
        P("groups"),
    )
    out_specs = P(("groups", "blk"), None)
    return jax.shard_map(
        fused if fits(mesh) else per_device,
        mesh=mesh,
        in_specs=in_specs,
        out_specs=out_specs,
        check_vma=False,
    )
```

```python
import functools
import math

import jax
import jax.numpy as jnp
from jax import lax
from jax.experimental import pallas as pl
from jax.experimental.pallas import tpu as pltpu
from jax.sharding import PartitionSpec as P

H = 64
KVH = 4
HD = 128
REQ_TOK = 16
PAIR = 2


HIGHEST = lax.Precision.HIGHEST
NEG_FILL = -1e30


def head_partials(query_rows, first_row, keys_split, values_split, key_pos, lengths):
    row_count = query_rows.shape[0]
    kv_count = keys_split.shape[1]
    head_count = query_rows.shape[1] // HD
    grouped = query_rows.reshape(row_count, kv_count, head_count // kv_count, HD)
    scores = jnp.einsum(
        "tgje,pge->tgjp", grouped, keys_split, precision=HIGHEST, preferred_element_type=jnp.float32
    ) * (1.0 / math.sqrt(HD))
    request_ids = (first_row + jnp.arange(row_count, dtype=jnp.int32)) // REQ_TOK
    request_table = jnp.arange(lengths.shape[0], dtype=jnp.int32)
    limits = jnp.sum(
        jnp.where(request_ids[:, None] == request_table[None, :], lengths[None, :], 0), axis=1
    )
    visible = key_pos[None, :] < limits[:, None]
    visible_four = visible[:, None, None, :]
    masked = jnp.where(visible_four, scores, NEG_FILL)
    peak_vals = jnp.max(masked, axis=3)
    weights = jnp.where(visible_four, jnp.exp(masked - peak_vals[..., None]), 0.0)
    totals = jnp.sum(weights, axis=3)
    mixed_values = jnp.einsum(
        "tgjp,pge->tgje",
        weights,
        values_split,
        precision=HIGHEST,
        preferred_element_type=jnp.float32,
    )
    return (
        mixed_values.reshape(row_count, head_count * HD),
        peak_vals.reshape(row_count, head_count),
        totals.reshape(row_count, head_count),
    )


def visit_blocks(running, shard_rows, first_row, keys_split, values_split, key_pos, lengths):
    row_count = shard_rows.shape[0]
    step_rows = 32

    def advance(step_id, current):
        row_begin = first_row + step_id * step_rows
        rows_now = lax.dynamic_slice_in_dim(shard_rows, step_id * step_rows, step_rows, 0)
        parts_now = head_partials(rows_now, row_begin, keys_split, values_split, key_pos, lengths)
        return tuple(
            (
                lax.dynamic_update_slice_in_dim(whole_arr, piece_now, row_begin, 0)
                for whole_arr, piece_now in zip(current, parts_now)
            )
        )

    return lax.fori_loop(0, row_count // step_rows, advance, running)


def per_device(queries, prefix_keys, prefix_values, out_weight, lengths):
    blocks = lax.axis_size("blk")
    position = lax.axis_index("blk")
    local_rows = queries.shape[0]
    total_rows = local_rows * blocks
    feature_count = H * HD
    key_count = prefix_keys.shape[0]
    group_size = H // KVH
    sub_count = blocks // KVH
    sub_len = key_count // sub_count
    key_send = (
        prefix_keys.reshape(sub_count, sub_len, KVH, HD)
        .transpose(0, 2, 1, 3)
        .reshape(blocks, sub_len, HD)
    )
    value_send = (
        prefix_values.reshape(sub_count, sub_len, KVH, HD)
        .transpose(0, 2, 1, 3)
        .reshape(blocks, sub_len, HD)
    )
    held_keys, held_values = (
        lax.all_to_all(key_send, "blk", split_axis=0, concat_axis=0, tiled=True),
        lax.all_to_all(value_send, "blk", split_axis=0, concat_axis=0, tiled=True),
    )
    sub_index = position // KVH
    source_ids = jnp.arange(blocks, dtype=jnp.int32)
    held_pos = (
        source_ids[:, None] * key_count
        + sub_index * sub_len
        + jnp.arange(sub_len, dtype=jnp.int32)[None, :]
    ).reshape(blocks * sub_len)
    held_keys = held_keys.reshape(blocks * sub_len, 1, HD)
    held_values = held_values.reshape(blocks * sub_len, 1, HD)
    query_heads = queries.reshape(local_rows, KVH, group_size * HD).transpose(1, 0, 2)
    query_send = jnp.broadcast_to(
        query_heads[None], (sub_count, KVH, local_rows, group_size * HD)
    ).reshape(blocks, local_rows, group_size * HD)
    query_held = lax.all_to_all(query_send, "blk", split_axis=0, concat_axis=0, tiled=True).reshape(
        total_rows, group_size * HD
    )
    empty_heads = (
        jnp.zeros((total_rows, group_size * HD), jnp.float32),
        jnp.zeros((total_rows, group_size), jnp.float32),
        jnp.zeros((total_rows, group_size), jnp.float32),
    )
    part_sums, part_peaks, part_totals = visit_blocks(
        empty_heads, query_held, 0, held_keys, held_values, held_pos, lengths
    )
    back_sums, back_peaks, back_totals = (
        lax.all_to_all(part_sums, "blk", split_axis=0, concat_axis=0, tiled=True),
        lax.all_to_all(part_peaks, "blk", split_axis=0, concat_axis=0, tiled=True),
        lax.all_to_all(part_totals, "blk", split_axis=0, concat_axis=0, tiled=True),
    )
    sums_split = back_sums.reshape(sub_count, KVH, local_rows, group_size, HD)
    peaks_split = back_peaks.reshape(sub_count, KVH, local_rows, group_size)
    overall = jnp.max(peaks_split, axis=0)
    factor = jnp.exp(peaks_split - overall[None])
    numerator = jnp.sum(sums_split * factor[..., None], axis=0)
    denominator = jnp.sum(
        back_totals.reshape(sub_count, KVH, local_rows, group_size) * factor, axis=0
    )
    attended = (
        (numerator / denominator[..., None])
        .transpose(1, 0, 2, 3)
        .reshape(local_rows, feature_count)
    )
    feature_rows = lax.all_to_all(attended, "blk", split_axis=1, concat_axis=0, tiled=True)
    return lax.psum_scatter(
        jnp.dot(feature_rows, out_weight, precision=HIGHEST, preferred_element_type=jnp.float32),
        "blk",
        scatter_dimension=0,
        tiled=True,
    )

def split_two(values):
    high = values.astype(jnp.bfloat16)
    return high, (values - high.astype(jnp.float32)).astype(jnp.bfloat16)


def fused_kernel(
    planes,
    pieces,
    weight_parts,
    q_hbm,
    k_hbm,
    v_hbm,
    w_hbm,
    len_hbm,
    out_ref,
    len_ref,
    q_all,
    q_rows,
    k_all,
    v_all,
    scores,
    w_full,
    w_high,
    w_low,
    part_out,
    part_in,
    plane_out,
    pair_in,
    pair_out,
    plane_in,
    line_out,
    own_sem,
    w_sem,
    qz_send,
    qz_recv,
    qp_send,
    qp_recv,
    k_send,
    k_recv,
    v_send,
    v_recv,
    c_send,
    c_recv,
    p_send,
    p_recv,
    r_send,
    r_recv,
    l_send,
    l_recv,
    o_sem,
):
    me = lax.axis_index("blk")
    line = lax.div(me, planes)
    spot = lax.rem(me, planes)
    side, core = lax.div(spot, PAIR), lax.rem(spot, PAIR)
    sides = planes // PAIR
    group_size = H // KVH
    group_width = group_size * HD
    local_rows = q_hbm.shape[0]
    key_count = k_hbm.shape[0]
    tile_rows = KVH * local_rows
    row_total = planes * tile_rows
    own_heads = group_size // planes
    width = w_hbm.shape[1]

    def remote(src, dst, send, recv, target):
        return pltpu.make_async_remote_copy(
            src_ref=src,
            dst_ref=dst,
            send_sem=send,
            recv_sem=recv,
            device_id={"blk": target},
            device_id_type=pl.DeviceIdType.MESH,
        )

    def line_peer(step):
        return lax.rem(line + step, KVH)

    def plane_peer(step):
        return lax.rem(spot + step, planes)

    def head_cols(ref, head, size):
        return ref.at[:, pl.ds(pl.multiple_of(head * size, size), size)]

    line_steps = [2, 1, 3] if KVH == 4 else list(range(1, KVH))
    plane_steps = list(range(1, planes))

    own = [
        pltpu.make_async_copy(head_cols(q_hbm, line, group_width), q_all.at[spot, 0], own_sem.at[0]),
        pltpu.make_async_copy(head_cols(k_hbm, line, HD), k_all.at[0], own_sem.at[1]),
        pltpu.make_async_copy(head_cols(v_hbm, line, HD), v_all.at[0], own_sem.at[2]),
        pltpu.make_async_copy(len_hbm, len_ref, own_sem.at[3]),
    ]
    for copy in own:
        copy.start()
    w_step = w_hbm.shape[0] // weight_parts
    w_copies = [
        pltpu.make_async_copy(
            w_hbm.at[pl.ds(n * w_step, w_step)], w_full.at[pl.ds(n * w_step, w_step)], w_sem.at[n]
        )
        for n in range(weight_parts)
    ]
    for copy in w_copies:
        copy.start()

    barrier = pltpu.get_barrier_semaphore()
    for step in line_steps:
        pl.semaphore_signal(
            barrier,
            inc=1,
            device_id={"blk": line_peer(step) * planes + spot},
            device_id_type=pl.DeviceIdType.MESH,
        )
    for step in plane_steps:
        pl.semaphore_signal(
            barrier,
            inc=1,
            device_id={"blk": line * planes + plane_peer(step)},
            device_id_type=pl.DeviceIdType.MESH,
        )
    pl.semaphore_wait(barrier, len(line_steps) + len(plane_steps))

    q_line, k_line, v_line = {}, {}, {}
    for step in line_steps:
        head = line_peer(step)
        q_line[step] = remote(
            head_cols(q_hbm, head, group_width),
            q_all.at[spot, step],
            qz_send.at[step],
            qz_recv.at[step],
            head * planes + spot,
        )
        q_line[step].start()
    for source, target, send, recv, made in (
        (k_hbm, k_all, k_send, k_recv, k_line),
        (v_hbm, v_all, v_send, v_recv, v_line),
    ):
        for step in line_steps:
            head = line_peer(step)
            made[step] = remote(
                head_cols(source, head, HD),
                target.at[step],
                send.at[step],
                recv.at[step],
                head * planes + spot,
            )
            made[step].start()

    split_rows, split_cols = 16, width // 2

    def split_part(part):
        w_copies[part].wait()

        def body(at, carry):
            rows = pl.ds(pl.multiple_of(part * w_step + at * split_rows, split_rows), split_rows)
            for half in range(width // split_cols):
                cols = pl.ds(half * split_cols, split_cols)
                high, low = split_two(w_full[rows, cols])
                w_high[rows, cols] = high
                w_low[rows, cols] = low
            return carry

        lax.fori_loop(0, w_step // split_rows, body, 0)

    early = weight_parts // 2
    for part in range(early):
        split_part(part)

    own[0].wait()
    for step in line_steps:
        q_line[step].wait_recv()
    q_plane = {}
    for step in plane_steps:
        q_plane[step] = remote(
            q_all.at[spot],
            q_all.at[spot],
            qp_send.at[step],
            qp_recv.at[step],
            line * planes + plane_peer(step),
        )
        q_plane[step].start()
    for part in range(early, weight_parts):
        split_part(part)
    for step in plane_steps:
        q_plane[step].wait_recv()

    for place in range(planes):
        for step in range(KVH):
            first = place * tile_rows + step * local_rows
            for head in range(group_size):
                q_rows[pl.ds(head * row_total + first, local_rows), :] = q_all[
                    place, step, :, pl.ds(head * HD, HD)
                ]
    query = q_rows[...]

    columns = group_size * row_total
    lane = lax.broadcasted_iota(jnp.int32, (1, columns), 1) % row_total
    lane_line = (line - (lane % tile_rows) // local_rows + KVH) % KVH
    token = (lane_line * planes + lane // tile_rows) * local_rows + lane % local_rows
    request = token // REQ_TOK
    own[3].wait()
    limits = jnp.zeros((1, columns), jnp.int32)
    for n in range(len_ref.shape[0]):
        limits = jnp.where(request == n, len_ref[n], limits)

    def key_place(step):
        source = lax.rem(line - step + KVH, KVH) * planes + spot
        return source * key_count + lax.broadcasted_iota(jnp.int32, (key_count, 1), 0)

    scale = 1.0 / math.sqrt(HD)
    peak = None
    for step in [0] + line_steps:
        if step == 0:
            own[1].wait()
        else:
            k_line[step].wait_recv()
        block = (
            lax.dot_general(
                k_all[step],
                query,
                (((1,), (1,)), ((), ())),
                precision=HIGHEST,
                preferred_element_type=jnp.float32,
            )
            * scale
        )
        block = jnp.where(key_place(step) < limits, block, NEG_FILL)
        scores[step] = block
        top = jnp.max(block, axis=0, keepdims=True)
        peak = top if peak is None else jnp.maximum(peak, top)
    total = jnp.zeros((1, columns), jnp.float32)
    for step in range(KVH):
        weights = jnp.where(key_place(step) < limits, jnp.exp(scores[step] - peak), 0.0)
        total = total + jnp.sum(weights, axis=0, keepdims=True)
        scores[step] = weights
    sums = jnp.zeros((HD, columns), jnp.float32)
    for step in [0] + line_steps:
        if step == 0:
            own[2].wait()
        else:
            v_line[step].wait_recv()
        sums = sums + lax.dot_general(
            v_all[step],
            scores[step],
            (((0,), (0,)), ((), ())),
            precision=HIGHEST,
            preferred_element_type=jnp.float32,
        )

    part_cols = own_heads * row_total
    for place in range(planes):
        cols = slice(place * part_cols, (place + 1) * part_cols)
        part_out[place, pl.ds(0, HD), :] = sums[:, cols]
        part_out[place, pl.ds(HD, 1), :] = peak[:, cols]
        part_out[place, pl.ds(HD + 1, 1), :] = total[:, cols]
    combine = {}
    for step in plane_steps:
        place = plane_peer(step)
        combine[step] = remote(
            part_out.at[place],
            part_in.at[step],
            c_send.at[step],
            c_recv.at[step],
            line * planes + place,
        )
        combine[step].start()
    for step in plane_steps:
        combine[step].wait_recv()
    peaks = [part_out[spot, pl.ds(HD, 1), :]] + [part_in[n, pl.ds(HD, 1), :] for n in plane_steps]
    totals = [part_out[spot, pl.ds(HD + 1, 1), :]] + [
        part_in[n, pl.ds(HD + 1, 1), :] for n in plane_steps
    ]
    overall = functools.reduce(jnp.maximum, peaks)
    factors = [jnp.exp(value - overall) for value in peaks]
    denominator = sum(value * factor for value, factor in zip(totals, factors))
    numerator = part_out[spot, pl.ds(0, HD), :] * factors[0]
    for step in plane_steps:
        numerator = numerator + part_in[step, pl.ds(0, HD), :] * factors[step]
    attended = (numerator / denominator).T
    features = jnp.concatenate(
        [attended[n * row_total : (n + 1) * row_total] for n in range(own_heads)], axis=1
    )
    high, low = split_two(features)
    both = jnp.concatenate([high, low], axis=0)

    piece = width // pieces
    pair_copies, plane_copies, line_copies, own_out = [], [], [], []

    def project(n):
        cols = pl.ds(n * piece, piece)
        first = jnp.dot(both, w_high[:, cols], preferred_element_type=jnp.float32)
        second = jnp.dot(high, w_low[:, cols], preferred_element_type=jnp.float32)
        mixed = first[:row_total] + first[row_total:] + second
        for place in range(planes):
            plane_out[n, place % PAIR, place // PAIR] = mixed[
                place * tile_rows : (place + 1) * tile_rows
            ]
        made = {}
        for step in range(1, PAIR):
            other = lax.rem(core + step, PAIR)
            made[step] = remote(
                plane_out.at[n, other],
                pair_in.at[n, step],
                p_send.at[n, step],
                p_recv.at[n, step],
                line * planes + side * PAIR + other,
            )
            made[step].start()
        pair_copies.append(made)

    def add_pair(n):
        value = plane_out[n, core]
        for step in range(1, PAIR):
            pair_copies[n][step].wait_recv()
            value = value + pair_in[n, step]
        pair_out[n] = value
        made = {}
        for step in range(1, sides):
            other = lax.rem(side + step, sides)
            made[step] = remote(
                pair_out.at[n, other],
                plane_in.at[n, step],
                r_send.at[n, step],
                r_recv.at[n, step],
                line * planes + other * PAIR + core,
            )
            made[step].start()
        plane_copies.append(made)

    ahead = min(2, pieces)
    for n in range(pieces + ahead):
        if n < pieces:
            project(n)
        if n >= ahead:
            add_pair(n - ahead)

    for n in range(pieces):
        value = pair_out[n, side]
        for step in range(1, sides):
            plane_copies[n][step].wait_recv()
            value = value + plane_in[n, step]
        for step in range(KVH):
            line_out[n, step] = value[step * local_rows : (step + 1) * local_rows]
        own_out.append(
            pltpu.make_async_copy(
                line_out.at[n, 0], out_ref.at[0, :, pl.ds(n * piece, piece)], o_sem.at[n]
            )
        )
        own_out[n].start()
        made = {}
        for step in line_steps:
            target = lax.rem(line - step + KVH, KVH) * planes + spot
            made[step] = remote(
                line_out.at[n, step],
                out_ref.at[step, :, pl.ds(n * piece, piece)],
                l_send.at[n, step],
                l_recv.at[n, step],
                target,
            )
            made[step].start()
        line_copies.append(made)
    for n in range(pieces):
        own_out[n].wait()
        for step in line_steps:
            line_copies[n][step].wait_recv()

    for made in [q_line, k_line, v_line, q_plane, combine] + pair_copies + plane_copies + line_copies:
        for copy in made.values():
            copy.wait_send()


def fused(queries, prefix_keys, prefix_values, out_weight, lengths):
    blocks = lax.axis_size("blk")
    planes = blocks // KVH
    sides = planes // PAIR
    local_rows = queries.shape[0]
    key_count = prefix_keys.shape[0]
    depth, width = out_weight.shape
    group_size = H // KVH
    tile_rows = KVH * local_rows
    row_total = planes * tile_rows
    columns = group_size * row_total
    part_cols = columns // planes
    pieces, weight_parts = 4, 8
    piece = width // pieces
    f32 = jnp.float32
    any_space = pl.BlockSpec(memory_space=pltpu.HBM)
    sems = pltpu.SemaphoreType.DMA
    line_parts = pl.pallas_call(
        functools.partial(fused_kernel, planes, pieces, weight_parts),
        out_shape=jax.ShapeDtypeStruct((KVH, local_rows, width), f32),
        in_specs=[any_space] * 5,
        out_specs=any_space,
        scratch_shapes=[
            pltpu.SMEM(lengths.shape, lengths.dtype),
            pltpu.VMEM((planes, KVH, local_rows, group_size * HD), f32),
            pltpu.VMEM((columns, HD), f32),
            pltpu.VMEM((KVH, key_count, HD), f32),
            pltpu.VMEM((KVH, key_count, HD), f32),
            pltpu.VMEM((KVH, key_count, columns), f32),
            pltpu.VMEM((depth, width), f32),
            pltpu.VMEM((depth, width), jnp.bfloat16),
            pltpu.VMEM((depth, width), jnp.bfloat16),
            pltpu.VMEM((planes, HD + 8, part_cols), f32),
            pltpu.VMEM((planes, HD + 8, part_cols), f32),
            pltpu.VMEM((pieces, PAIR, sides, tile_rows, piece), f32),
            pltpu.VMEM((pieces, PAIR, sides, tile_rows, piece), f32),
            pltpu.VMEM((pieces, sides, tile_rows, piece), f32),
            pltpu.VMEM((pieces, sides, tile_rows, piece), f32),
            pltpu.VMEM((pieces, KVH, local_rows, piece), f32),
            sems((4,)),
            sems((weight_parts,)),
            sems((KVH,)),
            sems((KVH,)),
            sems((planes,)),
            sems((planes,)),
            sems((KVH,)),
            sems((KVH,)),
            sems((KVH,)),
            sems((KVH,)),
            sems((planes,)),
            sems((planes,)),
            sems((pieces, PAIR)),
            sems((pieces, PAIR)),
            sems((pieces, sides)),
            sems((pieces, sides)),
            sems((pieces, KVH)),
            sems((pieces, KVH)),
            sems((pieces,)),
        ],
        compiler_params=pltpu.CompilerParams(
            collective_id=0, has_side_effects=True, vmem_limit_bytes=64 * 1024 * 1024
        ),
    )(queries, prefix_keys, prefix_values, out_weight, lengths)
    return jnp.sum(line_parts, axis=0)


def fits(mesh):
    blocks = mesh.shape["blk"]
    if blocks % KVH or (H // KVH) % (blocks // KVH):
        return False
    planes = blocks // KVH
    return planes % PAIR == 0 and planes <= 8


def solution(mesh):
    in_specs = (
        P(("groups", "blk"), None),
        P(("groups", "blk"), None),
        P(("groups", "blk"), None),
        P("blk", None),
        P("groups"),
    )
    out_specs = P(("groups", "blk"), None)
    return jax.shard_map(
        fused if fits(mesh) else per_device,
        mesh=mesh,
        in_specs=in_specs,
        out_specs=out_specs,
        check_vma=False,
    )
```

```python
import functools
import math

import jax
import jax.numpy as jnp
from jax import lax
from jax.experimental import pallas as pl
from jax.experimental.pallas import tpu as pltpu
from jax.sharding import PartitionSpec as P

H = 64
KVH = 4
HD = 128
REQ_TOK = 16
PAIR = 2


HIGHEST = lax.Precision.HIGHEST
NEG_FILL = -1e30


def head_partials(query_rows, first_row, keys_split, values_split, key_pos, lengths):
    row_count = query_rows.shape[0]
    kv_count = keys_split.shape[1]
    head_count = query_rows.shape[1] // HD
    grouped = query_rows.reshape(row_count, kv_count, head_count // kv_count, HD)
    scores = jnp.einsum(
        "tgje,pge->tgjp", grouped, keys_split, precision=HIGHEST, preferred_element_type=jnp.float32
    ) * (1.0 / math.sqrt(HD))
    request_ids = (first_row + jnp.arange(row_count, dtype=jnp.int32)) // REQ_TOK
    request_table = jnp.arange(lengths.shape[0], dtype=jnp.int32)
    limits = jnp.sum(
        jnp.where(request_ids[:, None] == request_table[None, :], lengths[None, :], 0), axis=1
    )
    visible = key_pos[None, :] < limits[:, None]
    visible_four = visible[:, None, None, :]
    masked = jnp.where(visible_four, scores, NEG_FILL)
    peak_vals = jnp.max(masked, axis=3)
    weights = jnp.where(visible_four, jnp.exp(masked - peak_vals[..., None]), 0.0)
    totals = jnp.sum(weights, axis=3)
    mixed_values = jnp.einsum(
        "tgjp,pge->tgje",
        weights,
        values_split,
        precision=HIGHEST,
        preferred_element_type=jnp.float32,
    )
    return (
        mixed_values.reshape(row_count, head_count * HD),
        peak_vals.reshape(row_count, head_count),
        totals.reshape(row_count, head_count),
    )


def visit_blocks(running, shard_rows, first_row, keys_split, values_split, key_pos, lengths):
    row_count = shard_rows.shape[0]
    step_rows = 32

    def advance(step_id, current):
        row_begin = first_row + step_id * step_rows
        rows_now = lax.dynamic_slice_in_dim(shard_rows, step_id * step_rows, step_rows, 0)
        parts_now = head_partials(rows_now, row_begin, keys_split, values_split, key_pos, lengths)
        return tuple(
            (
                lax.dynamic_update_slice_in_dim(whole_arr, piece_now, row_begin, 0)
                for whole_arr, piece_now in zip(current, parts_now)
            )
        )

    return lax.fori_loop(0, row_count // step_rows, advance, running)


def per_device(queries, prefix_keys, prefix_values, out_weight, lengths):
    blocks = lax.axis_size("blk")
    position = lax.axis_index("blk")
    local_rows = queries.shape[0]
    total_rows = local_rows * blocks
    feature_count = H * HD
    key_count = prefix_keys.shape[0]
    group_size = H // KVH
    sub_count = blocks // KVH
    sub_len = key_count // sub_count
    key_send = (
        prefix_keys.reshape(sub_count, sub_len, KVH, HD)
        .transpose(0, 2, 1, 3)
        .reshape(blocks, sub_len, HD)
    )
    value_send = (
        prefix_values.reshape(sub_count, sub_len, KVH, HD)
        .transpose(0, 2, 1, 3)
        .reshape(blocks, sub_len, HD)
    )
    held_keys, held_values = (
        lax.all_to_all(key_send, "blk", split_axis=0, concat_axis=0, tiled=True),
        lax.all_to_all(value_send, "blk", split_axis=0, concat_axis=0, tiled=True),
    )
    sub_index = position // KVH
    source_ids = jnp.arange(blocks, dtype=jnp.int32)
    held_pos = (
        source_ids[:, None] * key_count
        + sub_index * sub_len
        + jnp.arange(sub_len, dtype=jnp.int32)[None, :]
    ).reshape(blocks * sub_len)
    held_keys = held_keys.reshape(blocks * sub_len, 1, HD)
    held_values = held_values.reshape(blocks * sub_len, 1, HD)
    query_heads = queries.reshape(local_rows, KVH, group_size * HD).transpose(1, 0, 2)
    query_send = jnp.broadcast_to(
        query_heads[None], (sub_count, KVH, local_rows, group_size * HD)
    ).reshape(blocks, local_rows, group_size * HD)
    query_held = lax.all_to_all(query_send, "blk", split_axis=0, concat_axis=0, tiled=True).reshape(
        total_rows, group_size * HD
    )
    empty_heads = (
        jnp.zeros((total_rows, group_size * HD), jnp.float32),
        jnp.zeros((total_rows, group_size), jnp.float32),
        jnp.zeros((total_rows, group_size), jnp.float32),
    )
    part_sums, part_peaks, part_totals = visit_blocks(
        empty_heads, query_held, 0, held_keys, held_values, held_pos, lengths
    )
    back_sums, back_peaks, back_totals = (
        lax.all_to_all(part_sums, "blk", split_axis=0, concat_axis=0, tiled=True),
        lax.all_to_all(part_peaks, "blk", split_axis=0, concat_axis=0, tiled=True),
        lax.all_to_all(part_totals, "blk", split_axis=0, concat_axis=0, tiled=True),
    )
    sums_split = back_sums.reshape(sub_count, KVH, local_rows, group_size, HD)
    peaks_split = back_peaks.reshape(sub_count, KVH, local_rows, group_size)
    overall = jnp.max(peaks_split, axis=0)
    factor = jnp.exp(peaks_split - overall[None])
    numerator = jnp.sum(sums_split * factor[..., None], axis=0)
    denominator = jnp.sum(
        back_totals.reshape(sub_count, KVH, local_rows, group_size) * factor, axis=0
    )
    attended = (
        (numerator / denominator[..., None])
        .transpose(1, 0, 2, 3)
        .reshape(local_rows, feature_count)
    )
    feature_rows = lax.all_to_all(attended, "blk", split_axis=1, concat_axis=0, tiled=True)
    return lax.psum_scatter(
        jnp.dot(feature_rows, out_weight, precision=HIGHEST, preferred_element_type=jnp.float32),
        "blk",
        scatter_dimension=0,
        tiled=True,
    )

def split_two(values):
    high = values.astype(jnp.bfloat16)
    return high, (values - high.astype(jnp.float32)).astype(jnp.bfloat16)


def fused_kernel(
    planes,
    pieces,
    weight_parts,
    q_hbm,
    k_hbm,
    v_hbm,
    w_hbm,
    len_hbm,
    out_ref,
    len_ref,
    q_all,
    q_rows,
    k_all,
    v_all,
    scores,
    w_full,
    w_high,
    w_low,
    part_out,
    part_in,
    plane_out,
    pair_in,
    pair_out,
    plane_in,
    line_out,
    own_sem,
    w_sem,
    qz_send,
    qz_recv,
    qp_send,
    qp_recv,
    k_send,
    k_recv,
    v_send,
    v_recv,
    c_send,
    c_recv,
    p_send,
    p_recv,
    r_send,
    r_recv,
    l_send,
    l_recv,
    o_sem,
):
    me = lax.axis_index("blk")
    line = lax.div(me, planes)
    spot = lax.rem(me, planes)
    side, core = lax.div(spot, PAIR), lax.rem(spot, PAIR)
    sides = planes // PAIR
    group_size = H // KVH
    group_width = group_size * HD
    local_rows = q_hbm.shape[0]
    key_count = k_hbm.shape[0]
    tile_rows = KVH * local_rows
    row_total = planes * tile_rows
    own_heads = group_size // planes
    width = w_hbm.shape[1]

    def remote(src, dst, send, recv, target):
        return pltpu.make_async_remote_copy(
            src_ref=src,
            dst_ref=dst,
            send_sem=send,
            recv_sem=recv,
            device_id={"blk": target},
            device_id_type=pl.DeviceIdType.MESH,
        )

    def line_peer(step):
        return lax.rem(line + step, KVH)

    def plane_peer(step):
        return lax.rem(spot + step, planes)

    def head_cols(ref, head, size):
        return ref.at[:, pl.ds(pl.multiple_of(head * size, size), size)]

    line_steps = [1, 3, 2] if KVH == 4 else list(range(1, KVH))
    plane_steps = list(range(1, planes))

    barrier = pltpu.get_barrier_semaphore()
    for step in line_steps:
        pl.semaphore_signal(
            barrier,
            inc=1,
            device_id={"blk": line_peer(step) * planes + spot},
            device_id_type=pl.DeviceIdType.MESH,
        )
    for step in plane_steps:
        pl.semaphore_signal(
            barrier,
            inc=1,
            device_id={"blk": line * planes + plane_peer(step)},
            device_id_type=pl.DeviceIdType.MESH,
        )
    own = [
        pltpu.make_async_copy(head_cols(q_hbm, line, group_width), q_all.at[spot, 0], own_sem.at[0]),
        pltpu.make_async_copy(head_cols(k_hbm, line, HD), k_all.at[0], own_sem.at[1]),
        pltpu.make_async_copy(head_cols(v_hbm, line, HD), v_all.at[0], own_sem.at[2]),
        pltpu.make_async_copy(len_hbm, len_ref, own_sem.at[3]),
    ]
    for copy in own:
        copy.start()
    w_step = w_hbm.shape[0] // weight_parts
    w_copies = [
        pltpu.make_async_copy(
            w_hbm.at[pl.ds(n * w_step, w_step)], w_full.at[pl.ds(n * w_step, w_step)], w_sem.at[n]
        )
        for n in range(weight_parts)
    ]
    pl.semaphore_wait(barrier, len(line_steps) + len(plane_steps))

    q_line, k_line, v_line = {}, {}, {}
    for step in line_steps:
        head = line_peer(step)
        q_line[step] = remote(
            head_cols(q_hbm, head, group_width),
            q_all.at[spot, step],
            qz_send.at[step],
            qz_recv.at[step],
            head * planes + spot,
        )
        q_line[step].start()
    for source, target, send, recv, made in (
        (k_hbm, k_all, k_send, k_recv, k_line),
        (v_hbm, v_all, v_send, v_recv, v_line),
    ):
        for step in line_steps:
            head = line_peer(step)
            made[step] = remote(
                head_cols(source, head, HD),
                target.at[step],
                send.at[step],
                recv.at[step],
                head * planes + spot,
            )
            made[step].start()

    for copy in w_copies:
        copy.start()

    split_rows, split_cols = 16, width // 2

    def split_part(part):
        w_copies[part].wait()

        def body(at, carry):
            rows = pl.ds(pl.multiple_of(part * w_step + at * split_rows, split_rows), split_rows)
            for half in range(width // split_cols):
                cols = pl.ds(half * split_cols, split_cols)
                high, low = split_two(w_full[rows, cols])
                w_high[rows, cols] = high
                w_low[rows, cols] = low
            return carry

        lax.fori_loop(0, w_step // split_rows, body, 0)

    early = weight_parts // 2
    for part in range(early):
        split_part(part)

    own[0].wait()
    for step in line_steps:
        q_line[step].wait_recv()
    q_plane = {}
    for step in plane_steps:
        q_plane[step] = remote(
            q_all.at[spot],
            q_all.at[spot],
            qp_send.at[step],
            qp_recv.at[step],
            line * planes + plane_peer(step),
        )
        q_plane[step].start()
    for part in range(early, weight_parts):
        split_part(part)
    for step in plane_steps:
        q_plane[step].wait_recv()

    for place in range(planes):
        for step in range(KVH):
            first = place * tile_rows + step * local_rows
            for head in range(group_size):
                q_rows[pl.ds(head * row_total + first, local_rows), :] = q_all[
                    place, step, :, pl.ds(head * HD, HD)
                ]
    query = q_rows[...]

    columns = group_size * row_total
    lane = lax.broadcasted_iota(jnp.int32, (1, columns), 1) % row_total
    lane_line = (line - (lane % tile_rows) // local_rows + KVH) % KVH
    token = (lane_line * planes + lane // tile_rows) * local_rows + lane % local_rows
    request = token // REQ_TOK
    own[3].wait()
    limits = jnp.zeros((1, columns), jnp.int32)
    for n in range(len_ref.shape[0]):
        limits = jnp.where(request == n, len_ref[n], limits)

    def key_place(step):
        source = lax.rem(line - step + KVH, KVH) * planes + spot
        return source * key_count + lax.broadcasted_iota(jnp.int32, (key_count, 1), 0)

    scale = 1.0 / math.sqrt(HD)
    peak = None
    for step in [0] + line_steps:
        if step == 0:
            own[1].wait()
        else:
            k_line[step].wait_recv()
        block = (
            lax.dot_general(
                k_all[step],
                query,
                (((1,), (1,)), ((), ())),
                precision=HIGHEST,
                preferred_element_type=jnp.float32,
            )
            * scale
        )
        block = jnp.where(key_place(step) < limits, block, NEG_FILL)
        scores[step] = block
        top = jnp.max(block, axis=0, keepdims=True)
        peak = top if peak is None else jnp.maximum(peak, top)
    total = jnp.zeros((1, columns), jnp.float32)
    for step in range(KVH):
        weights = jnp.where(key_place(step) < limits, jnp.exp(scores[step] - peak), 0.0)
        total = total + jnp.sum(weights, axis=0, keepdims=True)
        scores[step] = weights
    sums = jnp.zeros((HD, columns), jnp.float32)
    for step in [0] + line_steps:
        if step == 0:
            own[2].wait()
        else:
            v_line[step].wait_recv()
        sums = sums + lax.dot_general(
            v_all[step],
            scores[step],
            (((0,), (0,)), ((), ())),
            precision=HIGHEST,
            preferred_element_type=jnp.float32,
        )

    part_cols = own_heads * row_total
    for place in range(planes):
        cols = slice(place * part_cols, (place + 1) * part_cols)
        part_out[place, pl.ds(0, HD), :] = sums[:, cols]
        part_out[place, pl.ds(HD, 1), :] = peak[:, cols]
        part_out[place, pl.ds(HD + 1, 1), :] = total[:, cols]
    combine = {}
    for step in plane_steps:
        place = plane_peer(step)
        combine[step] = remote(
            part_out.at[place],
            part_in.at[step],
            c_send.at[step],
            c_recv.at[step],
            line * planes + place,
        )
        combine[step].start()
    for step in plane_steps:
        combine[step].wait_recv()
    peaks = [part_out[spot, pl.ds(HD, 1), :]] + [part_in[n, pl.ds(HD, 1), :] for n in plane_steps]
    totals = [part_out[spot, pl.ds(HD + 1, 1), :]] + [
        part_in[n, pl.ds(HD + 1, 1), :] for n in plane_steps
    ]
    overall = functools.reduce(jnp.maximum, peaks)
    factors = [jnp.exp(value - overall) for value in peaks]
    denominator = sum(value * factor for value, factor in zip(totals, factors))
    numerator = part_out[spot, pl.ds(0, HD), :] * factors[0]
    for step in plane_steps:
        numerator = numerator + part_in[step, pl.ds(0, HD), :] * factors[step]
    attended = (numerator / denominator).T
    features = jnp.concatenate(
        [attended[n * row_total : (n + 1) * row_total] for n in range(own_heads)], axis=1
    )
    high, low = split_two(features)
    both = jnp.concatenate([high, low], axis=0)

    piece = width // pieces
    pair_copies, plane_copies, line_copies, own_out = [], [], [], []

    def project(n):
        cols = pl.ds(n * piece, piece)
        first = jnp.dot(both, w_high[:, cols], preferred_element_type=jnp.float32)
        second = jnp.dot(high, w_low[:, cols], preferred_element_type=jnp.float32)
        mixed = first[:row_total] + first[row_total:] + second
        for place in range(planes):
            plane_out[n, place % PAIR, place // PAIR] = mixed[
                place * tile_rows : (place + 1) * tile_rows
            ]
        made = {}
        for step in range(1, PAIR):
            other = lax.rem(core + step, PAIR)
            made[step] = remote(
                plane_out.at[n, other],
                pair_in.at[n, step],
                p_send.at[n, step],
                p_recv.at[n, step],
                line * planes + side * PAIR + other,
            )
            made[step].start()
        pair_copies.append(made)

    def add_pair(n):
        value = plane_out[n, core]
        for step in range(1, PAIR):
            pair_copies[n][step].wait_recv()
            value = value + pair_in[n, step]
        pair_out[n] = value
        made = {}
        for step in range(1, sides):
            other = lax.rem(side + step, sides)
            made[step] = remote(
                pair_out.at[n, other],
                plane_in.at[n, step],
                r_send.at[n, step],
                r_recv.at[n, step],
                line * planes + other * PAIR + core,
            )
            made[step].start()
        plane_copies.append(made)

    ahead = min(2, pieces)
    for n in range(pieces + ahead):
        if n < pieces:
            project(n)
        if n >= ahead:
            add_pair(n - ahead)

    for n in range(pieces):
        value = pair_out[n, side]
        for step in range(1, sides):
            plane_copies[n][step].wait_recv()
            value = value + plane_in[n, step]
        for step in range(KVH):
            line_out[n, step] = value[step * local_rows : (step + 1) * local_rows]
        own_out.append(
            pltpu.make_async_copy(
                line_out.at[n, 0], out_ref.at[0, :, pl.ds(n * piece, piece)], o_sem.at[n]
            )
        )
        own_out[n].start()
        made = {}
        for step in line_steps:
            target = lax.rem(line - step + KVH, KVH) * planes + spot
            made[step] = remote(
                line_out.at[n, step],
                out_ref.at[step, :, pl.ds(n * piece, piece)],
                l_send.at[n, step],
                l_recv.at[n, step],
                target,
            )
            made[step].start()
        line_copies.append(made)
    for n in range(pieces):
        own_out[n].wait()
        for step in line_steps:
            line_copies[n][step].wait_recv()

    for made in [q_line, k_line, v_line, q_plane, combine] + pair_copies + plane_copies + line_copies:
        for copy in made.values():
            copy.wait_send()


def fused(queries, prefix_keys, prefix_values, out_weight, lengths):
    blocks = lax.axis_size("blk")
    planes = blocks // KVH
    sides = planes // PAIR
    local_rows = queries.shape[0]
    key_count = prefix_keys.shape[0]
    depth, width = out_weight.shape
    group_size = H // KVH
    tile_rows = KVH * local_rows
    row_total = planes * tile_rows
    columns = group_size * row_total
    part_cols = columns // planes
    pieces, weight_parts = 4, 8
    piece = width // pieces
    f32 = jnp.float32
    any_space = pl.BlockSpec(memory_space=pltpu.HBM)
    sems = pltpu.SemaphoreType.DMA
    line_parts = pl.pallas_call(
        functools.partial(fused_kernel, planes, pieces, weight_parts),
        out_shape=jax.ShapeDtypeStruct((KVH, local_rows, width), f32),
        in_specs=[any_space] * 5,
        out_specs=any_space,
        scratch_shapes=[
            pltpu.SMEM(lengths.shape, lengths.dtype),
            pltpu.VMEM((planes, KVH, local_rows, group_size * HD), f32),
            pltpu.VMEM((columns, HD), f32),
            pltpu.VMEM((KVH, key_count, HD), f32),
            pltpu.VMEM((KVH, key_count, HD), f32),
            pltpu.VMEM((KVH, key_count, columns), f32),
            pltpu.VMEM((depth, width), f32),
            pltpu.VMEM((depth, width), jnp.bfloat16),
            pltpu.VMEM((depth, width), jnp.bfloat16),
            pltpu.VMEM((planes, HD + 8, part_cols), f32),
            pltpu.VMEM((planes, HD + 8, part_cols), f32),
            pltpu.VMEM((pieces, PAIR, sides, tile_rows, piece), f32),
            pltpu.VMEM((pieces, PAIR, sides, tile_rows, piece), f32),
            pltpu.VMEM((pieces, sides, tile_rows, piece), f32),
            pltpu.VMEM((pieces, sides, tile_rows, piece), f32),
            pltpu.VMEM((pieces, KVH, local_rows, piece), f32),
            sems((4,)),
            sems((weight_parts,)),
            sems((KVH,)),
            sems((KVH,)),
            sems((planes,)),
            sems((planes,)),
            sems((KVH,)),
            sems((KVH,)),
            sems((KVH,)),
            sems((KVH,)),
            sems((planes,)),
            sems((planes,)),
            sems((pieces, PAIR)),
            sems((pieces, PAIR)),
            sems((pieces, sides)),
            sems((pieces, sides)),
            sems((pieces, KVH)),
            sems((pieces, KVH)),
            sems((pieces,)),
        ],
        compiler_params=pltpu.CompilerParams(
            collective_id=0, has_side_effects=True, vmem_limit_bytes=64 * 1024 * 1024
        ),
    )(queries, prefix_keys, prefix_values, out_weight, lengths)
    return jnp.sum(line_parts, axis=0)


def fits(mesh):
    blocks = mesh.shape["blk"]
    if blocks % KVH or (H // KVH) % (blocks // KVH):
        return False
    planes = blocks // KVH
    return planes % PAIR == 0 and planes <= 8


def solution(mesh):
    in_specs = (
        P(("groups", "blk"), None),
        P(("groups", "blk"), None),
        P(("groups", "blk"), None),
        P("blk", None),
        P("groups"),
    )
    out_specs = P(("groups", "blk"), None)
    return jax.shard_map(
        fused if fits(mesh) else per_device,
        mesh=mesh,
        in_specs=in_specs,
        out_specs=out_specs,
        check_vma=False,
    )
```
